1024 devices in a mesh: wide: 16 (over y, core), narrow: 64 (over z, x).
Axes of the slice: x: 4, y: 8, z: 16, core: 2. Of those that a mesh axis runs over, the one named last changes fastest.
Arguments:
- forcing: float32 [512, 2048, 128], P('wide', 'narrow'), may hold values from -8 to 8
- classes: int32 [512, 2048], P('wide', 'narrow'), may hold values from 0 to 3
- drag: float32 [4], replicated, may hold values from 0.02 to 50
- depth: float32 [128], replicated, may hold values from 0.5 to 2
Outputs:
- pressure: float32 [512, 2048, 128], P('wide', 'narrow')
The draws below stay inside these ranges and needn't reach their ends.
All inputs are finite; a program needn't handle non-finite values.
Results may differ from the reference program's by a relative error of at most 0.0001.
Values sent between devices are 32-bit elements; how exact they have to be, the bound alone decides.
A program may use at most 32 MiB of HBM per device.

```python
import math
import jax
import jax.numpy as jnp
from jax import lax

CX = 32
CY = 32
NZ = 128
NCLASS = 4
NX = 512
NY = 2048
N_WIDE = 16
N_NARROW = 64


def draw_forcing(key, part):
    inner = jax.random.fold_in(key, 11)
    xs = jnp.arange(NX, dtype=jnp.float32) / NX
    ys = jnp.arange(NY, dtype=jnp.float32) / NY
    wave = jnp.sin(2.0 * math.pi * xs)[:, None] * jnp.cos(2.0 * math.pi * ys)[None, :]
    rough = jax.random.truncated_normal(inner, -6.0, 6.0, (NX, NY, NZ), jnp.float32)
    smooth = 0.002 + 0.001 * wave
    return (rough + smooth[:, :, None]).astype(jnp.float32)


def draw_classes(key, part):
    tile_key = jax.random.fold_in(key, 21)
    cell_key = jax.random.fold_in(key, 22)
    pick_key = jax.random.fold_in(key, 23)
    tiles = jax.random.randint(tile_key, (NX // CX, NY // CY), 0, NCLASS)
    spread = jnp.repeat(jnp.repeat(tiles, CX, axis=0), CY, axis=1)
    other = jax.random.randint(cell_key, (NX, NY), 0, NCLASS)
    pick = jax.random.randint(pick_key, (NX, NY), 0, 8)
    return jnp.where(pick == 0, other, spread).astype(jnp.int32)


def draw_drag(key, part):
    inner = jax.random.fold_in(key, 31)
    offset = jax.random.uniform(inner, (NCLASS,), jnp.float32, 0.0, 1.0)
    levels = jnp.arange(NCLASS, dtype=jnp.float32)
    base = 0.02 * jnp.exp(levels * math.log(10.0))
    return (base * jnp.exp(offset * math.log(2.5))).astype(jnp.float32)


def setup_inputs(seed: int = 0) -> dict:
    seeds = jax.random.split(jax.random.key(seed), 5)
    forcing = draw_forcing(jax.random.fold_in(seeds[4], 71), 0)
    classes = draw_classes(jax.random.fold_in(seeds[4], 71), 0)
    drag = draw_drag(jax.random.fold_in(seeds[4], 71), 0)
    depth = jnp.clip(jnp.exp(jax.random.uniform(seeds[3], (NZ,), jnp.float32, math.log(0.5), math.log(2.0))), 0.5, 2.0)
    return {"forcing": forcing, "classes": classes, "drag": drag, "depth": depth}


relax = 0.8

def vertical_terms(depth):
    coupling = 2.0 / (depth[:-1] + depth[1:])
    zero = jnp.zeros((1,), depth.dtype)
    return (jnp.concatenate([coupling, zero]), jnp.concatenate([zero, coupling]))

def apply_padded(padded, drag_cells, depth, upper, lower):
    centre = padded[1:-1, 1:-1]
    horiz = 4.0 * centre - padded[2:, 1:-1] - padded[:-2, 1:-1] - padded[1:-1, 2:] - padded[1:-1, :-2]
    zero = jnp.zeros(centre.shape[:2] + (1,), centre.dtype)
    above = jnp.concatenate([centre[:, :, 1:], zero], axis=2)
    below = jnp.concatenate([zero, centre[:, :, :-1]], axis=2)
    return depth * (horiz + drag_cells[:, :, None] * centre) + upper * (centre - above) + lower * (centre - below)

def coarse_solve(rhs, tile_drag, cx, cy):
    blocks = rhs.shape[1]
    rows = jnp.arange(blocks)[:, None]
    cols = jnp.arange(blocks)[None, :]
    eye = jnp.where(rows == cols, 1.0, 0.0).astype(jnp.float32)
    beside = jnp.where(jnp.abs(rows - cols) == 1, 1.0, 0.0).astype(jnp.float32)
    base = (2.0 * cx + 2.0 * cy) * eye - cx * beside

    def forward(carry, item):
        inv_prev, g_prev = carry
        rhs_row, drag_row = item
        block = base + eye * drag_row[None, :] - cy * cy * inv_prev
        g_now = rhs_row + cy * jnp.dot(inv_prev, g_prev, precision=lax.Precision.HIGHEST)
        factor = jnp.linalg.cholesky(block)
        half = lax.linalg.triangular_solve(factor, eye, left_side=True, lower=True)
        inverse = lax.linalg.triangular_solve(factor, half, left_side=True, lower=True, transpose_a=True)
        return ((inverse, g_now), (inverse, g_now))
    start = (jnp.zeros((blocks, blocks), jnp.float32), jnp.zeros((blocks,), jnp.float32))
    _, (inverses, g_all) = lax.scan(forward, start, (rhs, tile_drag))

    def backward(e_next, item):
        inverse, g_now = item
        e_now = jnp.dot(inverse, g_now + cy * e_next, precision=lax.Precision.HIGHEST)
        return (e_now, e_now)
    _, solved = lax.scan(backward, jnp.zeros((blocks,), jnp.float32), (inverses, g_all), reverse=True)
    return solved

def reference(forcing, classes, drag, depth):
    drag_cells = drag[classes]
    upper, lower = vertical_terms(depth)
    diag = depth * (4.0 + drag_cells[:, :, None]) + upper + lower

    def operate(field):
        padded = jnp.pad(field, ((1, 1), (1, 1), (0, 0)))
        return apply_padded(padded, drag_cells, depth, upper, lower)

    def sweep(field):
        return field + relax * (forcing - operate(field)) / diag
    first = relax * forcing / diag
    second = sweep(first)
    residual = forcing - operate(second)
    ztotal = jnp.sum(depth)
    tile_res = residual.reshape(N_WIDE, CX, N_NARROW, CY, NZ).sum(axis=(1, 3, 4))
    tile_drag = drag_cells.reshape(N_WIDE, CX, N_NARROW, CY).sum(axis=(1, 3)) / (CX * CY)
    correction = coarse_solve(tile_res / ztotal, tile_drag, CX, CY)
    spread = jnp.repeat(jnp.repeat(correction, CX, axis=0), CY, axis=1)
    corrected = second + spread[:, :, None]
    third = sweep(corrected)
    return sweep(third)
```

```python
import math
import functools
import jax
import jax.numpy as jnp
from jax import lax
from jax.experimental import pallas as pl
from jax.experimental.pallas import tpu as pltpu
from jax.sharding import PartitionSpec as P

f32 = jnp.float32
MESH = pl.DeviceIdType.MESH
ROWS = 1024
PAD = 32
CHUNK = 256
NW, NN = 16, 64

RHO = 32.0 * (2.0 * math.cos(math.pi / 17) + 2.0 * math.cos(math.pi / 65)) / 128.0199
HALF = 1.0 - RHO * RHO / 2.0
RHO2 = RHO * RHO / 2.0 / HALF
ROOT = math.sqrt(1.0 - RHO2 * RHO2)
SIG = (1.0 - ROOT) / RHO2
SCALE = 2.0 / (HALF * ROOT)
TRIPS = 16


def iota(shape, dim):
    return lax.broadcasted_iota(jnp.int32, shape, dim)


def layer(ref, side, base=0):
    if side == 0:
        return ref[pl.ds(base, 32), :]
    if side == 1:
        return ref[pl.ds(base + ROWS - 32, 32), :]
    return ref[pl.ds(base + (0 if side == 2 else 31), 32, stride=32), :]


def add_layer(ref, side, value, base=0):
    if side == 0:
        ref[pl.ds(base, 32), :] = ref[pl.ds(base, 32), :] + value
    elif side == 1:
        at = base + ROWS - 32
        ref[pl.ds(at, 32), :] = ref[pl.ds(at, 32), :] + value
    else:
        at = base + (0 if side == 2 else 31)
        ref[pl.ds(at, 32, stride=32), :] = ref[pl.ds(at, 32, stride=32), :] + value


CORNERS = ((0, 2), (0, 3), (1, 2), (1, 3))
CORNER_ROW = (0, 31, ROWS - 32, ROWS - 1)


def coarse_factor(d_ref, w0, n0):
    lane, sub = iota((8, 128), 1), iota((8, 128), 0)
    z, r = lane // 8, lane % 8
    q = {}
    for c in range(4):
        for p in range(2):
            q[c, p] = 32.0 / (128.0 + d_ref[pl.ds(8 * p + c, 8, stride=16), :])

    def shifted(v, cols):
        if cols == 0:
            return v
        rolled = pltpu.roll(v, (-8 * cols) % 128, 1)
        inside = (z + cols >= 0) & (z + cols < 16)
        return jnp.where(inside, rolled, 0.0)

    for c in list(range(-8, 0)) + list(range(4, 12)):
        for p in range(2):
            q[c, p] = shifted(q[c % 4, p], c // 4)

    def gather(x, c, p):
        other = x[c, 1 - p]
        if p == 0:
            near = jnp.where(sub == 0, 0.0, pltpu.roll(other, 1, 0))
        else:
            near = jnp.where(sub == 7, 0.0, pltpu.roll(other, 7, 0))
        return (x[c - 1, p] + x[c + 1, p]) + (other + near)

    dw = jnp.where(r == 0, -1, jnp.where(r == 1, 1, jnp.where(r < 4, 0, jnp.where(r < 6, -1, 1))))
    dn = jnp.where(r < 2, 0, jnp.where(r == 2, -1, jnp.where(r == 3, 1, jnp.where(r % 2 == 0, -1, 1))))
    want_w, want_n = w0 + dw, n0 + dn - 4 * z

    def unit(c, p):
        hit = (2 * sub + p == want_w) & (want_n == c)
        return jnp.where(hit, q[c, p] * (1.0 / 32.0), 0.0)

    def color(c, which):
        return (c + which) % 2

    b = {}
    for c in range(-1, 5):
        b[c, color(c, 1)] = unit(c, color(c, 1))
    g = {}
    for c in range(4):
        p = color(c, 0)
        g[c] = unit(c, p) + q[c, p] * gather(b, c, p)

    c_two, c_cur, c_old = 4.0 * SIG / (RHO * RHO), 2.0 * SIG, SIG * SIG

    def trip(it, carry):
        acc, cur, old = carry
        x, o = {}, {}
        for c in range(-8, 12):
            x[c, color(c, 0)] = shifted(cur[c % 4], c // 4)
            if -6 <= c < 10:
                o[c] = shifted(old[c % 4], c // 4)
        acc = list(acc)
        first = jnp.where(it == 0, 0.5, 1.0).astype(f32)
        for app in range(4):
            lo, hi = -8 + 2 * app, 12 - 2 * app
            y = {}
            for c in range(lo + 1, hi - 1):
                p = color(c, 1)
                y[c, p] = q[c, p] * gather(x, c, p)
            new = {}
            for c in range(lo + 2, hi - 2):
                p = color(c, 0)
                t = (c_two * q[c, p]) * gather(y, c, p) - c_cur * x[c, p]
                if app == 0:
                    t = first * t
                new[c, p] = t - c_old * o[c]
            o = {c: x[c, color(c, 0)] for c in range(lo + 2, hi - 2)}
            x = new
            for c in range(4):
                acc[c] = acc[c] + x[c, color(c, 0)]
        return tuple(acc), tuple(x[c, color(c, 0)] for c in range(4)), tuple(o[c] for c in range(4))

    g = tuple(g[c] for c in range(4))
    zero = jnp.zeros((8, 128), f32)
    acc, _, _ = lax.fori_loop(0, TRIPS, trip, (tuple(0.5 * v for v in g), g, (zero,) * 4))
    x = {(c, color(c, 0)): SCALE * acc[c] for c in range(4)}
    x[-1, color(-1, 0)] = shifted(x[3, color(3, 0)], -1)
    x[4, color(4, 0)] = shifted(x[0, color(0, 0)], 1)
    out = {}
    for c in range(4):
        out[c, color(c, 0)] = x[c, color(c, 0)]
        p = color(c, 1)
        out[c, p] = b[c, p] + q[c, p] * gather(x, c, p)
    return out


def kernel(
    f_ref, cls_ref, drag_ref, depth_ref, out_ref,
    r_ref, s_ref, v0_ref, v1_ref,
    row, ga1, ga2, gb1, gb2, snd_a, rcv_a, snd_b, rcv_b, dsnd, drcv,
    gs, gr, hs, hr, ds, dr,
):
    w0, n0 = lax.axis_index("wide"), lax.axis_index("narrow")
    z0, x0 = n0 // 4, n0 % 4

    bar = pltpu.get_barrier_semaphore()

    def greet_narrow(p, _):
        pl.semaphore_signal(bar, inc=1, device_id=(w0, (n0 + p) % NN), device_id_type=MESH)
        return 0

    def greet_wide(p, _):
        pl.semaphore_signal(bar, inc=1, device_id=((w0 + p) % NW, n0), device_id_type=MESH)
        return 0

    sides = (
        ((w0 + NW - 1) % NW, n0),
        ((w0 + 1) % NW, n0),
        (w0, (n0 + NN - 1) % NN),
        (w0, (n0 + 1) % NN),
    )
    diags = tuple((sides[a][0], sides[b][1]) for a, b in CORNERS)
    for t in diags:
        pl.semaphore_signal(bar, inc=1, device_id=t, device_id_type=MESH)
    lax.fori_loop(1, NN, greet_narrow, 0)
    lax.fori_loop(1, NW, greet_wide, 0)

    exist = (w0 > 0, w0 < NW - 1, n0 > 0, n0 < NN - 1)

    lane = iota((1, 128), 1)
    depth = depth_ref[...]
    link = jnp.where(lane == 127, 0.0, 2.0 / (depth + pltpu.roll(depth, 127, 1)))
    up, down = link, pltpu.roll(link, 1, 1)
    ztotal = jnp.sum(depth, axis=1, keepdims=True)
    drags = [drag_ref[c] for c in range(4)]
    tables = [0.8 / (depth * (4.0 + d) + up + down) for d in drags]

    kinds = cls_ref[...]
    s2d = jnp.where(kinds == 0, drags[0], jnp.where(kinds == 1, drags[1], jnp.where(kinds == 2, drags[2], drags[3])))
    own_drag = jnp.sum(jnp.sum(s2d, axis=0, keepdims=True), axis=1, keepdims=True) * (1.0 / ROWS)
    row[0:1, :] = jnp.broadcast_to(own_drag, (1, 128))

    pl.semaphore_wait(bar, (NN - 1) + (NW - 1) + 4)

    sub16, lane16 = iota((16, 128), 0), iota((16, 128), 1)
    mine = x0 * 16 + z0

    def gather_start(k, buf):
        def send(p, _):
            pltpu.make_async_remote_copy(
                src_ref=row.at[pl.ds(8 * k, 1)], dst_ref=buf.at[pl.ds(mine, 1)], send_sem=gs.at[2 * k],
                recv_sem=gr.at[2 * k], device_id=(w0, (n0 + p) % NN), device_id_type=MESH,
            ).start()
            return 0

        lax.fori_loop(1, NN, send, 0)
        buf[pl.ds(mine, 1), :] = row[8 * k : 8 * k + 1, :]

    def drain(buf, rows, sem):
        pltpu.make_async_copy(buf.at[pl.ds(0, rows)], buf.at[pl.ds(0, rows)], sem).wait()

    def gather_middle(k, buf, buf2):
        drain(buf, NN - 1, gr.at[2 * k])
        at = pl.multiple_of(w0 * 8, 8)
        rows = [
            jnp.sum(jnp.where(lane16 // 8 == sub16, buf[16 * x : 16 * x + 16, :], 0.0), axis=0, keepdims=True)
            for x in range(4)
        ]
        buf2[pl.ds(at, 8), :] = jnp.concatenate(rows + rows, axis=0)

        def send(p, _):
            pltpu.make_async_remote_copy(
                src_ref=buf2.at[pl.ds(at, 8)], dst_ref=buf2.at[pl.ds(at, 8)], send_sem=gs.at[2 * k + 1],
                recv_sem=gr.at[2 * k + 1], device_id=((w0 + p) % NW, n0), device_id_type=MESH,
            ).start()
            return 0

        lax.fori_loop(1, NW, send, 0)

    def gather_end(k, buf2):
        drain(buf2, 8 * (NW - 1), gr.at[2 * k + 1])

    def gather_close(k, buf, buf2):
        drain(buf, NN - 1, gs.at[2 * k])
        drain(buf2, 8 * (NW - 1), gs.at[2 * k + 1])

    gather_start(0, ga1)

    cf = kinds.astype(f32)
    eye = jnp.where(iota((32, 32), 0) == iota((32, 32), 1), 1.0, 0.0).astype(f32)
    ones = jnp.ones((32, 128), f32)
    zpad = jnp.zeros((PAD, 128), f32)
    for ref in (v0_ref, v1_ref):
        ref[0:PAD, :] = zpad
        ref[PAD + ROWS : PAD + ROWS + PAD, :] = zpad
    sum_f = jnp.zeros((8, 128), f32)
    for k in range(ROWS // CHUNK):
        ni = CHUNK // 32
        spread = (cf[k * ni : (k + 1) * ni][:, None, :] * eye[None]).reshape(CHUNK, 32)
        kind = jnp.dot(spread, ones, preferred_element_type=f32)
        is0, is1, is2 = kind < 0.5, kind < 1.5, kind < 2.5
        rr = jnp.where(is0, tables[0], jnp.where(is1, tables[1], jnp.where(is2, tables[2], tables[3])))
        ss = jnp.where(is0, drags[0], jnp.where(is1, drags[1], jnp.where(is2, drags[2], drags[3])))
        f = f_ref[k * CHUNK : (k + 1) * CHUNK, :]
        r_ref[k * CHUNK : (k + 1) * CHUNK, :] = rr
        s_ref[k * CHUNK : (k + 1) * CHUNK, :] = ss
        v0_ref[PAD + k * CHUNK : PAD + (k + 1) * CHUNK, :] = rr * f
        sum_f = sum_f + jnp.sum(f.reshape(CHUNK // 8, 8, 128), axis=0)

    jpos = iota((CHUNK, 128), 0) % 32

    def sweep(src, k):
        lo = k * CHUNK
        c = src[PAD + lo : PAD + lo + CHUNK, :]
        near = src[lo : lo + CHUNK, :] + src[2 * PAD + lo : 2 * PAD + lo + CHUNK, :]
        near = near + jnp.where(jpos == 0, 0.0, src[PAD + lo - 1 : PAD + lo - 1 + CHUNK, :])
        near = near + jnp.where(jpos == 31, 0.0, src[PAD + lo + 1 : PAD + lo + 1 + CHUNK, :])
        vert = up * pltpu.roll(c, 127, 1) + down * pltpu.roll(c, 1, 1)
        rr, f = r_ref[lo : lo + CHUNK, :], f_ref[lo : lo + CHUNK, :]
        return 0.2 * c + rr * (f + (depth * near + vert))

    sum_s = jnp.zeros((8, 128), f32)
    for k in range(ROWS // CHUNK):
        lo = k * CHUNK
        v = sweep(v0_ref, k)
        v1_ref[PAD + lo : PAD + lo + CHUNK, :] = v
        sum_s = sum_s + jnp.sum((s_ref[lo : lo + CHUNK, :] * v).reshape(CHUNK // 8, 8, 128), axis=0)

    def exchange(snd, rcv, base, corner_src):
        copies = []
        for side, t in enumerate(sides):
            copies.append(
                pltpu.make_async_remote_copy(
                    src_ref=snd.at[side], dst_ref=rcv.at[side ^ 1], send_sem=hs.at[base + side],
                    recv_sem=hr.at[base + (side ^ 1)], device_id=t, device_id_type=MESH,
                )
            )
        for corner, t in enumerate(diags):
            slot = base // 4
            dsnd[slot, corner, 0:1, :] = corner_src[PAD + CORNER_ROW[corner] : PAD + CORNER_ROW[corner] + 1, :]
            copies.append(
                pltpu.make_async_remote_copy(
                    src_ref=dsnd.at[slot, corner], dst_ref=drcv.at[slot, 3 - corner], send_sem=ds.at[base + corner],
                    recv_sem=dr.at[base + 3 - corner], device_id=t, device_id_type=MESH,
                )
            )
        for c in copies:
            c.start()
        return copies

    edge_sum = jnp.zeros((1, 128), f32)
    for side in range(4):
        snd_a[side, 0:32, :] = layer(v0_ref, side, PAD)
        snd_a[side, 32:64, :] = layer(r_ref, side)
        total = jnp.sum(layer(v1_ref, side, PAD), axis=0, keepdims=True)
        edge_sum = edge_sum + total
        snd_a[side, 64:72, :] = jnp.broadcast_to(total, (8, 128))
    sent_a = exchange(snd_a, rcv_a, 0, v0_ref)

    gather_middle(0, ga1, ga2)

    for c in sent_a:
        c.wait_recv()
    present = [jnp.where(e, 1.0, 0.0).astype(f32) for e in exist]
    r_out = [rcv_a[side, 32:64, :] * present[side] for side in range(4)]
    w_out = [depth * r_out[side] for side in range(4)]
    w_in = [depth * layer(r_ref, side) for side in range(4)]
    sub32 = iota((32, 128), 0)
    ends = jnp.where((sub32 == 0) | (sub32 == 31), 2.0, 1.0)
    flux = sum_s_row = jnp.sum(sum_s, axis=0, keepdims=True) + edge_sum
    deltas = []
    for side in range(4):
        delta = w_in[side] * (rcv_a[side, 0:32, :] * present[side])
        deltas.append(delta)
        term = (layer(s_ref, side) + ends) * delta - w_out[side] * layer(v0_ref, side, PAD)
        flux = flux + jnp.sum(term, axis=0, keepdims=True) - rcv_a[side, 64:65, :] * present[side]
    corner_first = []
    for corner, (a, b) in enumerate(CORNERS):
        at_a, at_b = 31 * (b - 2), 31 * a
        both = present[a] * present[b]
        value = drcv[0, corner, 0:1, :] * both
        flux = flux - (w_out[a][at_a : at_a + 1] + w_out[b][at_b : at_b + 1]) * value
    res = jnp.sum(sum_f, axis=0, keepdims=True) - depth * flux
    own_res = jnp.sum(res, axis=1, keepdims=True)
    row[8:9, :] = jnp.broadcast_to(own_res, (1, 128))
    gather_start(1, gb1)

    for side in range(4):
        add_layer(v1_ref, side, deltas[side], PAD)
    for k in range(ROWS // CHUNK):
        v0_ref[PAD + k * CHUNK : PAD + (k + 1) * CHUNK, :] = sweep(v1_ref, k)
    for side in range(4):
        snd_b[side, 0:32, :] = layer(v1_ref, side, PAD)
        snd_b[side, 32:64, :] = layer(v0_ref, side, PAD)
    sent_b = exchange(snd_b, rcv_b, 4, v1_ref)

    gather_end(0, ga2)
    columns = coarse_factor(ga2, w0, n0)
    gather_middle(1, gb1, gb2)

    for c in sent_b:
        c.wait_recv()
    outside = []
    for side in range(4):
        add_layer(v0_ref, side, w_in[side] * (rcv_b[side, 0:32, :] * present[side]), PAD)
        third = rcv_b[side, 32:64, :] * present[side] + w_out[side] * layer(v1_ref, side, PAD)
        outside.append(third)
    tips = []
    for side in range(4):
        lo_corner = (0, 2, 0, 1)[side]
        hi_corner = (1, 3, 2, 3)[side]
        pair = []
        for corner in (lo_corner, hi_corner):
            a, b = CORNERS[corner]
            pair.append(drcv[1, corner, 0:1, :] * (present[a] * present[b]))
        tip = jnp.where(sub32 == 0, pair[0], jnp.where(sub32 == 31, pair[1], 0.0))
        outside[side] = outside[side] + w_out[side] * tip

    gather_end(1, gb2)
    total = jnp.zeros((8, 128), f32)
    for c in range(4):
        for p in range(2):
            total = total + columns[c, p] * gb2[pl.ds(8 * p + c, 8, stride=16), :]
    line = jnp.sum(total, axis=0, keepdims=True)
    line = jnp.where(iota((8, 128), 1) % 8 == iota((8, 128), 0), line, 0.0)
    near = jnp.sum(line, axis=1, keepdims=True) / ztotal
    near = jnp.broadcast_to(near, (8, 128))
    e = [near[k : k + 1, :] for k in range(8)]
    e0 = (own_res / ztotal + 32.0 * (e[0] + e[1] + e[2] + e[3])) / (128.0 + own_drag)
    level = 4.0 * depth + up + down
    for side in range(4):
        add_layer(v0_ref, side, w_in[side] * (e[side] - e0), PAD)
        lo_corner = (0, 2, 0, 1)[side]
        hi_corner = (1, 3, 2, 3)[side]
        jump = jnp.where(
            sub32 == 0, e[4 + lo_corner] - e[side], jnp.where(sub32 == 31, e[4 + hi_corner] - e[side], 0.0)
        )
        own = (0.2 * present[side] + r_out[side] * level) * e[side]
        outside[side] = outside[side] + own + w_out[side] * ((e0 - e[side]) + jump)
    for k in range(ROWS // CHUNK):
        lo = k * CHUNK
        v1_ref[PAD + lo : PAD + lo + CHUNK, :] = v0_ref[PAD + lo : PAD + lo + CHUNK, :] + (
            0.2 + r_ref[lo : lo + CHUNK, :] * level
        ) * e0
    for k in range(ROWS // CHUNK):
        lo = k * CHUNK
        out_ref[lo : lo + CHUNK, :] = sweep(v1_ref, k)
    for side in range(4):
        add_layer(out_ref, side, w_in[side] * outside[side])

    for c in sent_a + sent_b:
        c.wait_send()
    gather_close(0, ga1, ga2)
    gather_close(1, gb1, gb2)


def local(forcing, classes, drag, depth):
    vmem, smem = pl.BlockSpec(memory_space=pltpu.VMEM), pl.BlockSpec(memory_space=pltpu.SMEM)
    field = pltpu.VMEM((ROWS, 128), f32)
    padded = pltpu.VMEM((ROWS + 2 * PAD, 128), f32)
    out = pl.pallas_call(
        kernel,
        out_shape=jax.ShapeDtypeStruct((ROWS, 128), f32),
        in_specs=[vmem, vmem, smem, vmem],
        out_specs=vmem,
        scratch_shapes=[
            field, field, padded, padded,
            pltpu.VMEM((16, 128), f32),
            pltpu.VMEM((NN, 128), f32), pltpu.VMEM((8 * NW, 128), f32),
            pltpu.VMEM((NN, 128), f32), pltpu.VMEM((8 * NW, 128), f32),
            pltpu.VMEM((4, 72, 128), f32), pltpu.VMEM((4, 72, 128), f32),
            pltpu.VMEM((4, 64, 128), f32), pltpu.VMEM((4, 64, 128), f32),
            pltpu.VMEM((2, 4, 8, 128), f32), pltpu.VMEM((2, 4, 8, 128), f32),
            pltpu.SemaphoreType.DMA((4,)), pltpu.SemaphoreType.DMA((4,)),
            pltpu.SemaphoreType.DMA((8,)), pltpu.SemaphoreType.DMA((8,)),
            pltpu.SemaphoreType.DMA((8,)), pltpu.SemaphoreType.DMA((8,)),
        ],
        compiler_params=pltpu.CompilerParams(
            collective_id=0, has_side_effects=True, vmem_limit_bytes=40 * 1024 * 1024
        ),
        name="vcycle",
    )(forcing.reshape(ROWS, 128), classes, drag, depth.reshape(1, 128))
    return out.reshape(forcing.shape)


def solution(mesh):
    in_specs = (P("wide", "narrow", None), P("wide", "narrow"), P(), P())
    out_specs = P("wide", "narrow", None)
    return jax.shard_map(local, mesh=mesh, in_specs=in_specs, out_specs=out_specs, check_vma=False)
```

```python
import math
import functools
import jax
import jax.numpy as jnp
from jax import lax
from jax.experimental import pallas as pl
from jax.experimental.pallas import tpu as pltpu
from jax.sharding import PartitionSpec as P

f32 = jnp.float32
MESH = pl.DeviceIdType.MESH
ROWS = 1024
PAD = 32
CHUNK = 256
NW, NN = 16, 64

RHO = 32.0 * (2.0 * math.cos(math.pi / 17) + 2.0 * math.cos(math.pi / 65)) / 128.0199
HALF = 1.0 - RHO * RHO / 2.0
RHO2 = RHO * RHO / 2.0 / HALF
ROOT = math.sqrt(1.0 - RHO2 * RHO2)
SIG = (1.0 - ROOT) / RHO2
SCALE = 2.0 / (HALF * ROOT)
TRIPS = 16


def iota(shape, dim):
    return lax.broadcasted_iota(jnp.int32, shape, dim)


def layer(ref, side, base=0):
    if side == 0:
        return ref[pl.ds(base, 32), :]
    if side == 1:
        return ref[pl.ds(base + ROWS - 32, 32), :]
    return ref[pl.ds(base + (0 if side == 2 else 31), 32, stride=32), :]


def add_layer(ref, side, value, base=0):
    if side == 0:
        ref[pl.ds(base, 32), :] = ref[pl.ds(base, 32), :] + value
    elif side == 1:
        at = base + ROWS - 32
        ref[pl.ds(at, 32), :] = ref[pl.ds(at, 32), :] + value
    else:
        at = base + (0 if side == 2 else 31)
        ref[pl.ds(at, 32, stride=32), :] = ref[pl.ds(at, 32, stride=32), :] + value


CORNERS = ((0, 2), (0, 3), (1, 2), (1, 3))
CORNER_ROW = (0, 31, ROWS - 32, ROWS - 1)


def coarse_factor(d_ref, w0, n0):
    lane, sub = iota((8, 128), 1), iota((8, 128), 0)
    z, r = lane // 8, lane % 8
    q = {}
    for c in range(4):
        for p in range(2):
            q[c, p] = 32.0 / (128.0 + d_ref[pl.ds(8 * p + c, 8, stride=16), :])

    def shifted(v, cols):
        if cols == 0:
            return v
        rolled = pltpu.roll(v, (-8 * cols) % 128, 1)
        inside = (z + cols >= 0) & (z + cols < 16)
        return jnp.where(inside, rolled, 0.0)

    for c in list(range(-8, 0)) + list(range(4, 12)):
        for p in range(2):
            q[c, p] = shifted(q[c % 4, p], c // 4)

    def gather(x, c, p):
        other = x[c, 1 - p]
        if p == 0:
            near = jnp.where(sub == 0, 0.0, pltpu.roll(other, 1, 0))
        else:
            near = jnp.where(sub == 7, 0.0, pltpu.roll(other, 7, 0))
        return (x[c - 1, p] + x[c + 1, p]) + (other + near)

    dw = jnp.where(r == 0, -1, jnp.where(r == 1, 1, jnp.where(r < 4, 0, jnp.where(r < 6, -1, 1))))
    dn = jnp.where(r < 2, 0, jnp.where(r == 2, -1, jnp.where(r == 3, 1, jnp.where(r % 2 == 0, -1, 1))))
    want_w, want_n = w0 + dw, n0 + dn - 4 * z

    def unit(c, p):
        hit = (2 * sub + p == want_w) & (want_n == c)
        return jnp.where(hit, q[c, p] * (1.0 / 32.0), 0.0)

    def color(c, which):
        return (c + which) % 2

    b = {}
    for c in range(-1, 5):
        b[c, color(c, 1)] = unit(c, color(c, 1))
    g = {}
    for c in range(4):
        p = color(c, 0)
        g[c] = unit(c, p) + q[c, p] * gather(b, c, p)

    c_two, c_cur, c_old = 4.0 * SIG / (RHO * RHO), 2.0 * SIG, SIG * SIG

    def trip(it, carry):
        acc, cur, old = carry
        x, o = {}, {}
        for c in range(-8, 12):
            x[c, color(c, 0)] = shifted(cur[c % 4], c // 4)
            if -6 <= c < 10:
                o[c] = shifted(old[c % 4], c // 4)
        acc = list(acc)
        first = jnp.where(it == 0, 0.5, 1.0).astype(f32)
        for app in range(4):
            lo, hi = -8 + 2 * app, 12 - 2 * app
            y = {}
            for c in range(lo + 1, hi - 1):
                p = color(c, 1)
                y[c, p] = q[c, p] * gather(x, c, p)
            new = {}
            for c in range(lo + 2, hi - 2):
                p = color(c, 0)
                t = (c_two * q[c, p]) * gather(y, c, p) - c_cur * x[c, p]
                if app == 0:
                    t = first * t
                new[c, p] = t - c_old * o[c]
            o = {c: x[c, color(c, 0)] for c in range(lo + 2, hi - 2)}
            x = new
            for c in range(4):
                acc[c] = acc[c] + x[c, color(c, 0)]
        return tuple(acc), tuple(x[c, color(c, 0)] for c in range(4)), tuple(o[c] for c in range(4))

    g = tuple(g[c] for c in range(4))
    zero = jnp.zeros((8, 128), f32)
    acc, _, _ = lax.fori_loop(0, TRIPS, trip, (tuple(0.5 * v for v in g), g, (zero,) * 4))
    x = {(c, color(c, 0)): SCALE * acc[c] for c in range(4)}
    x[-1, color(-1, 0)] = shifted(x[3, color(3, 0)], -1)
    x[4, color(4, 0)] = shifted(x[0, color(0, 0)], 1)
    out = {}
    for c in range(4):
        out[c, color(c, 0)] = x[c, color(c, 0)]
        p = color(c, 1)
        out[c, p] = b[c, p] + q[c, p] * gather(x, c, p)
    return out


def kernel(
    f_hbm, cls_hbm, drag_hbm, depth_hbm, out_hbm,
    f_ref, cls_ref, drag_ref, depth_ref,
    r_ref, s_ref, v0_ref, v1_ref, base_ref, unit_ref,
    row, ga1, ga2, gb1, gb2, snd_a, rcv_a, snd_b, rcv_b, dsnd, drcv,
    load, gs, gr, hs, hr, ds, dr, credit, store,
):
    w0, n0 = lax.axis_index("wide"), lax.axis_index("narrow")
    z0, x0 = n0 // 4, n0 % 4

    loads = [
        pltpu.make_async_copy(src, dst, load.at[k])
        for k, (src, dst) in enumerate(
            ((cls_hbm, cls_ref), (drag_hbm, drag_ref), (depth_hbm, depth_ref), (f_hbm, f_ref))
        )
    ]
    for c in loads:
        c.start()

    bar = pltpu.get_barrier_semaphore()

    def greet(w, n):
        pl.semaphore_signal(bar, inc=1, device_id=(w, n), device_id_type=MESH)

    def beside_x(p):
        return z0 * 4 + (x0 + p) % 4

    sides = ((w0 - 1, n0), (w0 + 1, n0), (w0, n0 - 1), (w0, n0 + 1))
    exist = (w0 > 0, w0 < NW - 1, n0 > 0, n0 < NN - 1)
    diags = tuple((sides[a][0], sides[b][1]) for a, b in CORNERS)
    dexist = tuple(exist[a] & exist[b] for a, b in CORNERS)

    def greet_wide(p, _):
        greet((w0 + p) % NW, n0)
        return 0

    def greet_above(n, _):
        greet(w0, n)
        return 0

    for p in range(1, 4):
        greet(w0, beside_x(p))
    for t, there in zip(diags, dexist):
        pl.when(there)(functools.partial(greet, *t))
    pl.when((x0 == 0) & (z0 > 0))(functools.partial(greet, w0, n0 - 1))
    lax.fori_loop(1, NW, greet_wide, 0)
    lax.fori_loop(4 * z0 + 4, NN, greet_above, 0)

    for side in range(4):

        @pl.when(jnp.logical_not(exist[side]))
        def _(side=side):
            rcv_a[side] = jnp.zeros((72, 128), f32)
            rcv_b[side] = jnp.zeros((64, 128), f32)

    for corner in range(4):

        @pl.when(jnp.logical_not(dexist[corner]))
        def _(corner=corner):
            drcv[0, corner] = jnp.zeros((8, 128), f32)
            drcv[1, corner] = jnp.zeros((8, 128), f32)

    zpad = jnp.zeros((PAD, 128), f32)
    for ref in (v0_ref, v1_ref):
        ref[0:PAD, :] = zpad
        ref[PAD + ROWS : PAD + ROWS + PAD, :] = zpad

    for c in loads[:3]:
        c.wait()
    lane = iota((1, 128), 1)
    depth = depth_ref[...]
    link = jnp.where(lane == 127, 0.0, 2.0 / (depth + pltpu.roll(depth, 127, 1)))
    up, down = link, pltpu.roll(link, 1, 1)
    ztotal = jnp.sum(depth, axis=1, keepdims=True)
    drags = [drag_ref[c] for c in range(4)]
    tables = [0.8 / (depth * (4.0 + d) + up + down) for d in drags]

    kinds = cls_ref[...]

    cf = kinds.astype(f32)
    eye = jnp.where(iota((32, 32), 0) == iota((32, 32), 1), 1.0, 0.0).astype(f32)
    ones = jnp.ones((32, 128), f32)
    loads[3].wait()
    sum_f = jnp.zeros((8, 128), f32)
    for k in range(ROWS // CHUNK):
        ni = CHUNK // 32
        spread = (cf[k * ni : (k + 1) * ni][:, None, :] * eye[None]).reshape(CHUNK, 32)
        kind = jnp.dot(spread, ones, preferred_element_type=f32)
        is0, is1, is2 = kind < 0.5, kind < 1.5, kind < 2.5
        rr = jnp.where(is0, tables[0], jnp.where(is1, tables[1], jnp.where(is2, tables[2], tables[3])))
        ss = jnp.where(is0, drags[0], jnp.where(is1, drags[1], jnp.where(is2, drags[2], drags[3])))
        f = f_ref[k * CHUNK : (k + 1) * CHUNK, :]
        r_ref[k * CHUNK : (k + 1) * CHUNK, :] = rr
        s_ref[k * CHUNK : (k + 1) * CHUNK, :] = ss
        v0_ref[PAD + k * CHUNK : PAD + (k + 1) * CHUNK, :] = rr * f
        sum_f = sum_f + jnp.sum(f.reshape(CHUNK // 8, 8, 128), axis=0)

    def sweep(src, lo, n, forced=True):
        jpos = iota((n, 128), 0) % 32
        c = src[PAD + lo : PAD + lo + n, :]
        near = src[lo : lo + n, :] + src[2 * PAD + lo : 2 * PAD + lo + n, :]
        near = near + jnp.where(jpos == 0, 0.0, src[PAD + lo - 1 : PAD + lo - 1 + n, :])
        near = near + jnp.where(jpos == 31, 0.0, src[PAD + lo + 1 : PAD + lo + 1 + n, :])
        force = depth * near + (up * pltpu.roll(c, 127, 1) + down * pltpu.roll(c, 1, 1))
        if forced:
            force = f_ref[lo : lo + n, :] + force
        return 0.2 * c + r_ref[lo : lo + n, :] * force

    def sweep_column(src, side):
        at = 0 if side == 2 else 31
        c = src[pl.ds(PAD + at, 32, stride=32), :]
        near = src[pl.ds(at, 32, stride=32), :] + src[pl.ds(2 * PAD + at, 32, stride=32), :]
        near = near + src[pl.ds(PAD + (1 if side == 2 else 30), 32, stride=32), :]
        force = depth * near + (up * pltpu.roll(c, 127, 1) + down * pltpu.roll(c, 1, 1))
        return 0.2 * c + layer(r_ref, side) * (layer(f_ref, side) + force)

    def exchange(snd, rcv, base, corner_src):
        copies = []
        for side, t in enumerate(sides):
            copy = pltpu.make_async_remote_copy(
                src_ref=snd.at[side], dst_ref=rcv.at[side ^ 1], send_sem=hs.at[base + side],
                recv_sem=hr.at[base + (side ^ 1)], device_id=t, device_id_type=MESH,
            )
            mirror = pltpu.make_async_remote_copy(
                src_ref=snd.at[side], dst_ref=rcv.at[side], send_sem=hs.at[base + side],
                recv_sem=hr.at[base + side], device_id=t, device_id_type=MESH,
            )
            copies.append((exist[side], copy, mirror))
        for corner, t in enumerate(diags):
            slot = base // 4
            dsnd[slot, corner, 0:1, :] = corner_src[PAD + CORNER_ROW[corner] : PAD + CORNER_ROW[corner] + 1, :]
            copy = pltpu.make_async_remote_copy(
                src_ref=dsnd.at[slot, corner], dst_ref=drcv.at[slot, 3 - corner], send_sem=ds.at[base + corner],
                recv_sem=dr.at[base + 3 - corner], device_id=t, device_id_type=MESH,
            )
            mirror = pltpu.make_async_remote_copy(
                src_ref=dsnd.at[slot, corner], dst_ref=drcv.at[slot, corner], send_sem=ds.at[base + corner],
                recv_sem=dr.at[base + corner], device_id=t, device_id_type=MESH,
            )
            copies.append((dexist[corner], copy, mirror))
        for there, copy, _ in copies:
            pl.when(there)(copy.start)
        return copies

    def arrive(copies):
        for there, _, mirror in copies:
            pl.when(there)(mirror.wait_recv)

    edge_sum = jnp.zeros((1, 128), f32)
    for side in range(4):
        snd_a[side, 0:32, :] = layer(v0_ref, side, PAD)
        snd_a[side, 32:64, :] = layer(r_ref, side)
        swept = sweep(v0_ref, (0, ROWS - 32)[side], 32) if side < 2 else sweep_column(v0_ref, side)
        total = jnp.sum(swept, axis=0, keepdims=True)
        edge_sum = edge_sum + total
        snd_a[side, 64:72, :] = jnp.broadcast_to(total, (8, 128))

    hello = 4 * z0 + 3 + (NW - 1) + jnp.where((x0 == 3) & (z0 < 15), 1, 0)
    for there in dexist:
        hello = hello + jnp.where(there, 1, 0)
    pl.semaphore_wait(bar, hello)

    sub16, lane16 = iota((16, 128), 0), iota((16, 128), 1)
    mine = x0 * 16 + z0

    def drain(buf, rows, sem):
        pltpu.make_async_copy(buf.at[pl.ds(0, rows)], buf.at[pl.ds(0, rows)], sem).wait()

    def narrow_send(k, buf, n):
        pltpu.make_async_remote_copy(
            src_ref=row.at[pl.ds(8 * k, 1)], dst_ref=buf.at[pl.ds(mine, 1)], send_sem=gs.at[2 * k],
            recv_sem=gr.at[2 * k], device_id=(w0, n), device_id_type=MESH,
        ).start()

    def gather_start(k, buf):
        buf[pl.ds(mine, 1), :] = row[8 * k : 8 * k + 1, :]

        def send(n, _):
            narrow_send(k, buf, n)
            return 0

        lax.fori_loop(0, 4 * z0, send, 0)
        for p in range(1, 4):
            narrow_send(k, buf, beside_x(p))

    def gather_above():
        @pl.when(z0 < 15)
        def _():
            pl.semaphore_wait(credit, 4 * (15 - z0))


        def send(n, _):
            narrow_send(0, ga1, n)
            narrow_send(1, gb1, n)
            return 0

        lax.fori_loop(4 * z0 + 4, NN, send, 0)

    def gather_middle(k, buf, buf2):
        drain(buf, NN - 1, gr.at[2 * k])
        at = pl.multiple_of(w0 * 8, 8)
        rows = [
            jnp.sum(jnp.where(lane16 // 8 == sub16, buf[16 * x : 16 * x + 16, :], 0.0), axis=0, keepdims=True)
            for x in range(4)
        ]
        buf2[pl.ds(at, 8), :] = jnp.concatenate(rows + rows, axis=0)

        def send(p, _):
            pltpu.make_async_remote_copy(
                src_ref=buf2.at[pl.ds(at, 8)], dst_ref=buf2.at[pl.ds(at, 8)], send_sem=gs.at[2 * k + 1],
                recv_sem=gr.at[2 * k + 1], device_id=((w0 + p) % NW, n0), device_id_type=MESH,
            ).start()
            return 0

        lax.fori_loop(1, NW, send, 0)

    def gather_end(k, buf2):
        drain(buf2, 8 * (NW - 1), gr.at[2 * k + 1])

    def gather_close(k, buf, buf2):
        drain(buf, NN - 1, gs.at[2 * k])
        drain(buf2, 8 * (NW - 1), gs.at[2 * k + 1])

    sent_a = exchange(snd_a, rcv_a, 0, v0_ref)
    s2d = jnp.where(kinds == 0, drags[0], jnp.where(kinds == 1, drags[1], jnp.where(kinds == 2, drags[2], drags[3])))
    own_drag = jnp.sum(jnp.sum(s2d, axis=0, keepdims=True), axis=1, keepdims=True) * (1.0 / ROWS)
    row[0:1, :] = jnp.broadcast_to(own_drag, (1, 128))
    gather_start(0, ga1)

    def give_credit(n, _):
        pl.semaphore_signal(credit, inc=1, device_id=(w0, n), device_id_type=MESH)
        return 0

    lax.fori_loop(0, 4 * z0, give_credit, 0)

    sum_s = jnp.zeros((8, 128), f32)
    for k in range(ROWS // CHUNK):
        lo = k * CHUNK
        v = sweep(v0_ref, lo, CHUNK)
        v1_ref[PAD + lo : PAD + lo + CHUNK, :] = v
        sum_s = sum_s + jnp.sum((s_ref[lo : lo + CHUNK, :] * v).reshape(CHUNK // 8, 8, 128), axis=0)

    arrive(sent_a)
    r_out = [rcv_a[side, 32:64, :] for side in range(4)]
    w_out = [depth * r_out[side] for side in range(4)]
    w_in = [depth * layer(r_ref, side) for side in range(4)]
    sub32 = iota((32, 128), 0)
    ends = jnp.where((sub32 == 0) | (sub32 == 31), 2.0, 1.0)
    flux = jnp.sum(sum_s, axis=0, keepdims=True) + edge_sum
    deltas = []
    for side in range(4):
        delta = w_in[side] * rcv_a[side, 0:32, :]
        deltas.append(delta)
        term = (layer(s_ref, side) + ends) * delta - w_out[side] * layer(v0_ref, side, PAD)
        flux = flux + jnp.sum(term, axis=0, keepdims=True) - rcv_a[side, 64:65, :]
    for corner, (a, b) in enumerate(CORNERS):
        at_a, at_b = 31 * (b - 2), 31 * a
        flux = flux - (w_out[a][at_a : at_a + 1] + w_out[b][at_b : at_b + 1]) * drcv[0, corner, 0:1, :]
    res = jnp.sum(sum_f, axis=0, keepdims=True) - depth * flux
    own_res = jnp.sum(res, axis=1, keepdims=True)
    row[8:9, :] = jnp.broadcast_to(own_res, (1, 128))
    gather_start(1, gb1)

    for side in range(4):
        add_layer(v1_ref, side, deltas[side], PAD)
    for k in range(ROWS // CHUNK):
        v0_ref[PAD + k * CHUNK : PAD + (k + 1) * CHUNK, :] = sweep(v1_ref, k * CHUNK, CHUNK)
    for side in range(4):
        snd_b[side, 0:32, :] = layer(v1_ref, side, PAD)
        snd_b[side, 32:64, :] = layer(v0_ref, side, PAD)
    sent_b = exchange(snd_b, rcv_b, 4, v1_ref)

    arrive(sent_b)
    outside = []
    for side in range(4):
        add_layer(v0_ref, side, w_in[side] * rcv_b[side, 0:32, :], PAD)
        outside.append(rcv_b[side, 32:64, :] + w_out[side] * layer(v1_ref, side, PAD))
    along = ((0, 1), (2, 3), (0, 2), (1, 3))
    for side in range(4):
        first, last = (drcv[1, corner, 0:1, :] for corner in along[side])
        tip = jnp.where(sub32 == 0, first, jnp.where(sub32 == 31, last, 0.0))
        outside[side] = outside[side] + w_out[side] * tip

    level = 4.0 * depth + up + down
    for k in range(ROWS // CHUNK):
        lo = k * CHUNK
        base_ref[lo : lo + CHUNK, :] = sweep(v0_ref, lo, CHUNK)
    for side in range(4):
        add_layer(base_ref, side, w_in[side] * outside[side])
    for k in range(ROWS // CHUNK):
        lo = k * CHUNK
        v1_ref[PAD + lo : PAD + lo + CHUNK, :] = 0.2 + r_ref[lo : lo + CHUNK, :] * level
    for k in range(ROWS // CHUNK):
        lo = k * CHUNK
        unit_ref[lo : lo + CHUNK, :] = sweep(v1_ref, lo, CHUNK, forced=False)
    w_next = [
        depth * r_ref[32:64, :],
        depth * r_ref[ROWS - 64 : ROWS - 32, :],
        depth * r_ref[pl.ds(1, 32, stride=32), :],
        depth * r_ref[pl.ds(30, 32, stride=32), :],
    ]

    gather_above()
    gather_middle(0, ga1, ga2)
    gather_middle(1, gb1, gb2)
    gather_end(0, ga2)
    columns = coarse_factor(ga2, w0, n0)

    gather_end(1, gb2)
    total = jnp.zeros((8, 128), f32)
    for c in range(4):
        for p in range(2):
            total = total + columns[c, p] * gb2[pl.ds(8 * p + c, 8, stride=16), :]
    line = jnp.sum(total, axis=0, keepdims=True)
    line = jnp.where(iota((8, 128), 1) % 8 == iota((8, 128), 0), line, 0.0)
    near = jnp.sum(line, axis=1, keepdims=True) / ztotal
    near = jnp.broadcast_to(near, (8, 128))
    e = [near[k : k + 1, :] for k in range(8)]
    e0 = (own_res / ztotal + 32.0 * (e[0] + e[1] + e[2] + e[3])) / (128.0 + own_drag)
    edge, inner = [], []
    for side in range(4):
        first, last = (e[4 + corner] - e[side] for corner in along[side])
        jump = jnp.where(sub32 == 0, first, jnp.where(sub32 == 31, last, 0.0))
        beyond = (0.2 + r_out[side] * level) * e[side] + w_out[side] * ((e0 - e[side]) + jump)
        d = w_in[side] * (e[side] - e0)
        near = jnp.where(sub32 == 0, 0.0, pltpu.roll(d, 1, 0)) + jnp.where(sub32 == 31, 0.0, pltpu.roll(d, 31, 0))
        vert = up * pltpu.roll(d, 127, 1) + down * pltpu.roll(d, 1, 1)
        edge.append(0.2 * d + w_in[side] * (near + beyond) + layer(r_ref, side) * vert)
        inner.append(w_next[side] * d)
    stores = []
    ni = CHUNK // 32
    for k in range(ROWS // CHUNK):
        lo = k * CHUNK
        base_ref[lo : lo + CHUNK, :] = base_ref[lo : lo + CHUNK, :] + e0 * unit_ref[lo : lo + CHUNK, :]
        if k == 0:
            base_ref[0:32, :] = base_ref[0:32, :] + edge[0]
            base_ref[32:64, :] = base_ref[32:64, :] + inner[0]
        if k == ROWS // CHUNK - 1:
            base_ref[ROWS - 32 : ROWS, :] = base_ref[ROWS - 32 : ROWS, :] + edge[1]
            base_ref[ROWS - 64 : ROWS - 32, :] = base_ref[ROWS - 64 : ROWS - 32, :] + inner[1]
        for at, part in ((0, edge[2]), (1, inner[2]), (31, edge[3]), (30, inner[3])):
            cells = pl.ds(lo + at, ni, stride=32)
            base_ref[cells, :] = base_ref[cells, :] + part[k * ni : (k + 1) * ni]
        stores.append(
            pltpu.make_async_copy(base_ref.at[pl.ds(lo, CHUNK)], out_hbm.at[pl.ds(lo, CHUNK)], store.at[k])
        )
        stores[-1].start()

    for c in stores:
        c.wait()
    for there, copy, _ in sent_a + sent_b:
        pl.when(there)(copy.wait_send)
    gather_close(0, ga1, ga2)
    gather_close(1, gb1, gb2)


def local(forcing, classes, drag, depth):
    hbm = pl.BlockSpec(memory_space=pltpu.HBM)
    field = pltpu.VMEM((ROWS, 128), f32)
    padded = pltpu.VMEM((ROWS + 2 * PAD, 128), f32)
    out = pl.pallas_call(
        kernel,
        out_shape=jax.ShapeDtypeStruct((ROWS, 128), f32),
        in_specs=[hbm] * 4,
        out_specs=hbm,
        scratch_shapes=[
            field, pltpu.VMEM((32, 32), jnp.int32), pltpu.SMEM((4,), f32), pltpu.VMEM((1, 128), f32),
            field, field, padded, padded, field, field,
            pltpu.VMEM((16, 128), f32),
            pltpu.VMEM((NN, 128), f32), pltpu.VMEM((8 * NW, 128), f32),
            pltpu.VMEM((NN, 128), f32), pltpu.VMEM((8 * NW, 128), f32),
            pltpu.VMEM((4, 72, 128), f32), pltpu.VMEM((4, 72, 128), f32),
            pltpu.VMEM((4, 64, 128), f32), pltpu.VMEM((4, 64, 128), f32),
            pltpu.VMEM((2, 4, 8, 128), f32), pltpu.VMEM((2, 4, 8, 128), f32),
            pltpu.SemaphoreType.DMA((4,)), pltpu.SemaphoreType.DMA((4,)), pltpu.SemaphoreType.DMA((4,)),
            pltpu.SemaphoreType.DMA((8,)), pltpu.SemaphoreType.DMA((8,)),
            pltpu.SemaphoreType.DMA((8,)), pltpu.SemaphoreType.DMA((8,)), pltpu.SemaphoreType.REGULAR,
            pltpu.SemaphoreType.DMA((ROWS // CHUNK,)),
        ],
        compiler_params=pltpu.CompilerParams(
            collective_id=0, has_side_effects=True, vmem_limit_bytes=58 * 1024 * 1024
        ),
        name="vcycle",
    )(forcing.reshape(ROWS, 128), classes, drag, depth.reshape(1, 128))
    return out.reshape(forcing.shape)


def solution(mesh):
    in_specs = (P("wide", "narrow", None), P("wide", "narrow"), P(), P())
    out_specs = P("wide", "narrow", None)
    return jax.shard_map(local, mesh=mesh, in_specs=in_specs, out_specs=out_specs, check_vma=False)
```

```python
import math
import functools
import jax
import jax.numpy as jnp
from jax import lax
from jax.experimental import pallas as pl
from jax.experimental.pallas import tpu as pltpu
from jax.sharding import PartitionSpec as P

f32 = jnp.float32
MESH = pl.DeviceIdType.MESH
ROWS = 1024
PAD = 32
CHUNK = 256
NW, NN = 16, 64

RHO = 32.0 * (2.0 * math.cos(math.pi / 17) + 2.0 * math.cos(math.pi / 65)) / 128.0199
HALF = 1.0 - RHO * RHO / 2.0
RHO2 = RHO * RHO / 2.0 / HALF
ROOT = math.sqrt(1.0 - RHO2 * RHO2)
SIG = (1.0 - ROOT) / RHO2
SCALE = 2.0 / (HALF * ROOT)
TRIPS = 16


def iota(shape, dim):
    return lax.broadcasted_iota(jnp.int32, shape, dim)


def layer(ref, side, base=0):
    if side == 0:
        return ref[pl.ds(base, 32), :]
    if side == 1:
        return ref[pl.ds(base + ROWS - 32, 32), :]
    return ref[pl.ds(base + (0 if side == 2 else 31), 32, stride=32), :]


def add_layer(ref, side, value, base=0):
    if side == 0:
        ref[pl.ds(base, 32), :] = ref[pl.ds(base, 32), :] + value
    elif side == 1:
        at = base + ROWS - 32
        ref[pl.ds(at, 32), :] = ref[pl.ds(at, 32), :] + value
    else:
        at = base + (0 if side == 2 else 31)
        ref[pl.ds(at, 32, stride=32), :] = ref[pl.ds(at, 32, stride=32), :] + value


CORNERS = ((0, 2), (0, 3), (1, 2), (1, 3))
CORNER_ROW = (0, 31, ROWS - 32, ROWS - 1)


def coarse_factor(d_ref, w0, n0):
    lane, sub = iota((8, 128), 1), iota((8, 128), 0)
    z, r = lane // 8, lane % 8
    q = {}
    for c in range(4):
        for p in range(2):
            q[c, p] = 32.0 / (128.0 + d_ref[pl.ds(8 * p + c, 8, stride=16), :])

    def shifted(v, cols):
        if cols == 0:
            return v
        rolled = pltpu.roll(v, (-8 * cols) % 128, 1)
        inside = (z + cols >= 0) & (z + cols < 16)
        return jnp.where(inside, rolled, 0.0)

    for c in list(range(-8, 0)) + list(range(4, 12)):
        for p in range(2):
            q[c, p] = shifted(q[c % 4, p], c // 4)

    def gather(x, c, p):
        other = x[c, 1 - p]
        if p == 0:
            near = jnp.where(sub == 0, 0.0, pltpu.roll(other, 1, 0))
        else:
            near = jnp.where(sub == 7, 0.0, pltpu.roll(other, 7, 0))
        return (x[c - 1, p] + x[c + 1, p]) + (other + near)

    dw = jnp.where(r == 0, -1, jnp.where(r == 1, 1, jnp.where(r < 4, 0, jnp.where(r < 6, -1, 1))))
    dn = jnp.where(r < 2, 0, jnp.where(r == 2, -1, jnp.where(r == 3, 1, jnp.where(r % 2 == 0, -1, 1))))
    want_w, want_n = w0 + dw, n0 + dn - 4 * z

    def unit(c, p):
        hit = (2 * sub + p == want_w) & (want_n == c)
        return jnp.where(hit, q[c, p] * (1.0 / 32.0), 0.0)

    def color(c, which):
        return (c + which) % 2

    b = {}
    for c in range(-1, 5):
        b[c, color(c, 1)] = unit(c, color(c, 1))
    g = {}
    for c in range(4):
        p = color(c, 0)
        g[c] = unit(c, p) + q[c, p] * gather(b, c, p)

    c_two, c_cur, c_old = 4.0 * SIG / (RHO * RHO), 2.0 * SIG, SIG * SIG

    def trip(it, carry):
        acc, cur, old = carry
        x, o = {}, {}
        for c in range(-8, 12):
            x[c, color(c, 0)] = shifted(cur[c % 4], c // 4)
            if -6 <= c < 10:
                o[c] = shifted(old[c % 4], c // 4)
        acc = list(acc)
        first = jnp.where(it == 0, 0.5, 1.0).astype(f32)
        for app in range(4):
            lo, hi = -8 + 2 * app, 12 - 2 * app
            y = {}
            for c in range(lo + 1, hi - 1):
                p = color(c, 1)
                y[c, p] = q[c, p] * gather(x, c, p)
            new = {}
            for c in range(lo + 2, hi - 2):
                p = color(c, 0)
                t = (c_two * q[c, p]) * gather(y, c, p) - c_cur * x[c, p]
                if app == 0:
                    t = first * t
                new[c, p] = t - c_old * o[c]
            o = {c: x[c, color(c, 0)] for c in range(lo + 2, hi - 2)}
            x = new
            for c in range(4):
                acc[c] = acc[c] + x[c, color(c, 0)]
        return tuple(acc), tuple(x[c, color(c, 0)] for c in range(4)), tuple(o[c] for c in range(4))

    g = tuple(g[c] for c in range(4))
    zero = jnp.zeros((8, 128), f32)
    acc, _, _ = lax.fori_loop(0, TRIPS, trip, (tuple(0.5 * v for v in g), g, (zero,) * 4))
    x = {(c, color(c, 0)): SCALE * acc[c] for c in range(4)}
    x[-1, color(-1, 0)] = shifted(x[3, color(3, 0)], -1)
    x[4, color(4, 0)] = shifted(x[0, color(0, 0)], 1)
    out = {}
    for c in range(4):
        out[c, color(c, 0)] = x[c, color(c, 0)]
        p = color(c, 1)
        out[c, p] = b[c, p] + q[c, p] * gather(x, c, p)
    return out


def kernel(
    f_hbm, cls_hbm, drag_hbm, depth_hbm, out_ref,
    f_ref, cls_ref, drag_ref, depth_ref,
    r_ref, s_ref, v0_ref, v1_ref, base_ref, unit_ref,
    row, ga1, ga2, gb1, gb2, snd_a, rcv_a, snd_b, rcv_b, dsnd, drcv,
    load, gs, gr, hs, hr, ds, dr, credit, ring,
):
    w0, n0 = lax.axis_index("wide"), lax.axis_index("narrow")
    z0, x0 = n0 // 4, n0 % 4

    loads = [
        pltpu.make_async_copy(src, dst, load.at[k])
        for k, (src, dst) in enumerate(
            ((cls_hbm, cls_ref), (drag_hbm, drag_ref), (depth_hbm, depth_ref), (f_hbm, f_ref))
        )
    ]
    for c in loads:
        c.start()

    bar = pltpu.get_barrier_semaphore()

    def greet(w, n):
        pl.semaphore_signal(bar, inc=1, device_id=(w, n), device_id_type=MESH)

    def beside_x(p):
        return z0 * 4 + (x0 + p) % 4

    sides = ((w0 - 1, n0), (w0 + 1, n0), (w0, n0 - 1), (w0, n0 + 1))
    exist = (w0 > 0, w0 < NW - 1, n0 > 0, n0 < NN - 1)
    diags = tuple((sides[a][0], sides[b][1]) for a, b in CORNERS)
    dexist = tuple(exist[a] & exist[b] for a, b in CORNERS)

    y0, c0 = w0 // 2, w0 % 2
    ring_next = (((y0 + 1) % 8) * 2 + c0, ((y0 + 7) % 8) * 2 + c0)

    def relay(k):
        for w in ring_next:
            pl.semaphore_signal(ring.at[k], inc=1, device_id=(w, n0), device_id_type=MESH)

    def greet_above(n, _):
        greet(w0, n)
        return 0

    for p in range(1, 4):
        greet(w0, beside_x(p))
    for t, there in zip(diags, dexist):
        pl.when(there)(functools.partial(greet, *t))
    pl.when((x0 == 0) & (z0 > 0))(functools.partial(greet, w0, n0 - 1))
    greet(y0 * 2 + (1 - c0), n0)
    for dy in (1, 7):
        for c in (0, 1):
            greet(((y0 + dy) % 8) * 2 + c, n0)
    lax.fori_loop(4 * z0 + 4, NN, greet_above, 0)

    for side in range(4):

        @pl.when(jnp.logical_not(exist[side]))
        def _(side=side):
            rcv_a[side] = jnp.zeros((72, 128), f32)
            rcv_b[side] = jnp.zeros((64, 128), f32)

    for corner in range(4):

        @pl.when(jnp.logical_not(dexist[corner]))
        def _(corner=corner):
            drcv[0, corner] = jnp.zeros((8, 128), f32)
            drcv[1, corner] = jnp.zeros((8, 128), f32)

    zpad = jnp.zeros((PAD, 128), f32)
    for ref in (v0_ref, v1_ref):
        ref[0:PAD, :] = zpad
        ref[PAD + ROWS : PAD + ROWS + PAD, :] = zpad

    for c in loads[:3]:
        c.wait()
    lane = iota((1, 128), 1)
    depth = depth_ref[...]
    link = jnp.where(lane == 127, 0.0, 2.0 / (depth + pltpu.roll(depth, 127, 1)))
    up, down = link, pltpu.roll(link, 1, 1)
    ztotal = jnp.sum(depth, axis=1, keepdims=True)
    drags = [drag_ref[c] for c in range(4)]
    tables = [0.8 / (depth * (4.0 + d) + up + down) for d in drags]

    kinds = cls_ref[...]

    cf = kinds.astype(f32)
    eye = jnp.where(iota((32, 32), 0) == iota((32, 32), 1), 1.0, 0.0).astype(f32)
    ones = jnp.ones((32, 128), f32)
    loads[3].wait()
    sum_f = jnp.zeros((8, 128), f32)
    for k in range(ROWS // CHUNK):
        ni = CHUNK // 32
        spread = (cf[k * ni : (k + 1) * ni][:, None, :] * eye[None]).reshape(CHUNK, 32)
        kind = jnp.dot(spread, ones, preferred_element_type=f32)
        is0, is1, is2 = kind < 0.5, kind < 1.5, kind < 2.5
        rr = jnp.where(is0, tables[0], jnp.where(is1, tables[1], jnp.where(is2, tables[2], tables[3])))
        ss = jnp.where(is0, drags[0], jnp.where(is1, drags[1], jnp.where(is2, drags[2], drags[3])))
        f = f_ref[k * CHUNK : (k + 1) * CHUNK, :]
        r_ref[k * CHUNK : (k + 1) * CHUNK, :] = rr
        s_ref[k * CHUNK : (k + 1) * CHUNK, :] = ss
        v0_ref[PAD + k * CHUNK : PAD + (k + 1) * CHUNK, :] = rr * f
        sum_f = sum_f + jnp.sum(f.reshape(CHUNK // 8, 8, 128), axis=0)

    def sweep(src, lo, n, forced=True):
        jpos = iota((n, 128), 0) % 32
        c = src[PAD + lo : PAD + lo + n, :]
        near = src[lo : lo + n, :] + src[2 * PAD + lo : 2 * PAD + lo + n, :]
        near = near + jnp.where(jpos == 0, 0.0, src[PAD + lo - 1 : PAD + lo - 1 + n, :])
        near = near + jnp.where(jpos == 31, 0.0, src[PAD + lo + 1 : PAD + lo + 1 + n, :])
        force = depth * near + (up * pltpu.roll(c, 127, 1) + down * pltpu.roll(c, 1, 1))
        if forced:
            force = f_ref[lo : lo + n, :] + force
        return 0.2 * c + r_ref[lo : lo + n, :] * force

    def sweep_column(src, side):
        at = 0 if side == 2 else 31
        c = src[pl.ds(PAD + at, 32, stride=32), :]
        near = src[pl.ds(at, 32, stride=32), :] + src[pl.ds(2 * PAD + at, 32, stride=32), :]
        near = near + src[pl.ds(PAD + (1 if side == 2 else 30), 32, stride=32), :]
        force = depth * near + (up * pltpu.roll(c, 127, 1) + down * pltpu.roll(c, 1, 1))
        return 0.2 * c + layer(r_ref, side) * (layer(f_ref, side) + force)

    def exchange(snd, rcv, base, corner_src):
        copies = []
        for side, t in enumerate(sides):
            copy = pltpu.make_async_remote_copy(
                src_ref=snd.at[side], dst_ref=rcv.at[side ^ 1], send_sem=hs.at[base + side],
                recv_sem=hr.at[base + (side ^ 1)], device_id=t, device_id_type=MESH,
            )
            mirror = pltpu.make_async_remote_copy(
                src_ref=snd.at[side], dst_ref=rcv.at[side], send_sem=hs.at[base + side],
                recv_sem=hr.at[base + side], device_id=t, device_id_type=MESH,
            )
            copies.append((exist[side], copy, mirror))
        for corner, t in enumerate(diags):
            slot = base // 4
            dsnd[slot, corner, 0:1, :] = corner_src[PAD + CORNER_ROW[corner] : PAD + CORNER_ROW[corner] + 1, :]
            copy = pltpu.make_async_remote_copy(
                src_ref=dsnd.at[slot, corner, pl.ds(0, 1)], dst_ref=drcv.at[slot, 3 - corner, pl.ds(0, 1)], send_sem=ds.at[base + corner],
                recv_sem=dr.at[base + 3 - corner], device_id=t, device_id_type=MESH,
            )
            mirror = pltpu.make_async_remote_copy(
                src_ref=dsnd.at[slot, corner, pl.ds(0, 1)], dst_ref=drcv.at[slot, corner, pl.ds(0, 1)], send_sem=ds.at[base + corner],
                recv_sem=dr.at[base + corner], device_id=t, device_id_type=MESH,
            )
            copies.append((dexist[corner], copy, mirror))
        for there, copy, _ in copies[4:] + copies[:4]:
            pl.when(there)(copy.start)
        return copies

    def arrive(copies):
        for there, _, mirror in copies:
            pl.when(there)(mirror.wait_recv)

    edge_sum = jnp.zeros((1, 128), f32)
    for side in range(4):
        snd_a[side, 0:32, :] = layer(v0_ref, side, PAD)
        snd_a[side, 32:64, :] = layer(r_ref, side)
        swept = sweep(v0_ref, (0, ROWS - 32)[side], 32) if side < 2 else sweep_column(v0_ref, side)
        total = jnp.sum(swept, axis=0, keepdims=True)
        edge_sum = edge_sum + total
        snd_a[side, 64:72, :] = jnp.broadcast_to(total, (8, 128))

    hello = 4 * z0 + 3 + 5 + jnp.where((x0 == 3) & (z0 < 15), 1, 0)
    for there in dexist:
        hello = hello + jnp.where(there, 1, 0)
    pl.semaphore_wait(bar, hello)
    relay(0)

    sub16, lane16 = iota((16, 128), 0), iota((16, 128), 1)
    mine = x0 * 16 + z0

    def drain(buf, rows, sem):
        pltpu.make_async_copy(buf.at[pl.ds(0, rows)], buf.at[pl.ds(0, rows)], sem).wait()

    def narrow_send(k, buf, n):
        pltpu.make_async_remote_copy(
            src_ref=row.at[pl.ds(8 * k, 1)], dst_ref=buf.at[pl.ds(mine, 1)], send_sem=gs.at[2 * k],
            recv_sem=gr.at[2 * k], device_id=(w0, n), device_id_type=MESH,
        ).start()

    def gather_start(k, buf):
        buf[pl.ds(mine, 1), :] = row[8 * k : 8 * k + 1, :]

        def send(n, _):
            narrow_send(k, buf, n)
            return 0

        lax.fori_loop(0, 4 * z0, send, 0)
        for p in range(1, 4):
            narrow_send(k, buf, beside_x(p))

    def gather_above():
        @pl.when(z0 < 15)
        def _():
            pl.semaphore_wait(credit, 4 * (15 - z0))


        def send(n, _):
            narrow_send(0, ga1, n)
            narrow_send(1, gb1, n)
            return 0

        lax.fori_loop(4 * z0 + 4, NN, send, 0)

    def gather_middle(k, buf, buf2):
        drain(buf, NN - 1, gr.at[2 * k])
        at = pl.multiple_of(w0 * 8, 8)
        rows = [
            jnp.sum(jnp.where(lane16 // 8 == sub16, buf[16 * x : 16 * x + 16, :], 0.0), axis=0, keepdims=True)
            for x in range(4)
        ]
        buf2[pl.ds(at, 4), :] = jnp.concatenate(rows, axis=0)

        def send(p, _):
            pltpu.make_async_remote_copy(
                src_ref=buf2.at[pl.ds(at, 4)], dst_ref=buf2.at[pl.ds(at, 4)], send_sem=gs.at[2 * k + 1],
                recv_sem=gr.at[2 * k + 1], device_id=((w0 + p) % NW, n0), device_id_type=MESH,
            ).start()
            return 0

        lax.fori_loop(1, NW, send, 0)

    def gather_end(k, buf2):
        drain(buf2, 4 * (NW - 1), gr.at[2 * k + 1])

    def gather_close(k, buf, buf2):
        drain(buf, NN - 1, gs.at[2 * k])
        drain(buf2, 4 * (NW - 1), gs.at[2 * k + 1])

    sent_a = exchange(snd_a, rcv_a, 0, v0_ref)
    s2d = jnp.where(kinds == 0, drags[0], jnp.where(kinds == 1, drags[1], jnp.where(kinds == 2, drags[2], drags[3])))
    own_drag = jnp.sum(jnp.sum(s2d, axis=0, keepdims=True), axis=1, keepdims=True) * (1.0 / ROWS)
    row[0:1, :] = jnp.broadcast_to(own_drag, (1, 128))
    gather_start(0, ga1)

    def give_credit(n, _):
        pl.semaphore_signal(credit, inc=1, device_id=(w0, n), device_id_type=MESH)
        return 0

    lax.fori_loop(0, 4 * z0, give_credit, 0)

    sum_s = jnp.zeros((8, 128), f32)
    for k in range(ROWS // CHUNK):
        lo = k * CHUNK
        v = sweep(v0_ref, lo, CHUNK)
        v1_ref[PAD + lo : PAD + lo + CHUNK, :] = v
        sum_s = sum_s + jnp.sum((s_ref[lo : lo + CHUNK, :] * v).reshape(CHUNK // 8, 8, 128), axis=0)

    pl.semaphore_wait(ring.at[0], 2)
    relay(1)
    arrive(sent_a)
    pl.semaphore_wait(ring.at[1], 2)
    relay(2)
    r_out = [rcv_a[side, 32:64, :] for side in range(4)]
    w_out = [depth * r_out[side] for side in range(4)]
    w_in = [depth * layer(r_ref, side) for side in range(4)]
    sub32 = iota((32, 128), 0)
    ends = jnp.where((sub32 == 0) | (sub32 == 31), 2.0, 1.0)
    flux = jnp.sum(sum_s, axis=0, keepdims=True) + edge_sum
    deltas = []
    for side in range(4):
        delta = w_in[side] * rcv_a[side, 0:32, :]
        deltas.append(delta)
        term = (layer(s_ref, side) + ends) * delta - w_out[side] * layer(v0_ref, side, PAD)
        flux = flux + jnp.sum(term, axis=0, keepdims=True) - rcv_a[side, 64:65, :]
    for corner, (a, b) in enumerate(CORNERS):
        at_a, at_b = 31 * (b - 2), 31 * a
        flux = flux - (w_out[a][at_a : at_a + 1] + w_out[b][at_b : at_b + 1]) * drcv[0, corner, 0:1, :]
    res = jnp.sum(sum_f, axis=0, keepdims=True) - depth * flux
    own_res = jnp.sum(res, axis=1, keepdims=True)
    row[8:9, :] = jnp.broadcast_to(own_res, (1, 128))
    gather_start(1, gb1)

    for side in range(4):
        add_layer(v1_ref, side, deltas[side], PAD)
    for k in range(ROWS // CHUNK):
        v0_ref[PAD + k * CHUNK : PAD + (k + 1) * CHUNK, :] = sweep(v1_ref, k * CHUNK, CHUNK)
    for side in range(4):
        snd_b[side, 0:32, :] = layer(v1_ref, side, PAD)
        snd_b[side, 32:64, :] = layer(v0_ref, side, PAD)
    sent_b = exchange(snd_b, rcv_b, 4, v1_ref)

    arrive(sent_b)
    outside = []
    for side in range(4):
        add_layer(v0_ref, side, w_in[side] * rcv_b[side, 0:32, :], PAD)
        outside.append(rcv_b[side, 32:64, :] + w_out[side] * layer(v1_ref, side, PAD))
    along = ((0, 1), (2, 3), (0, 2), (1, 3))
    for side in range(4):
        first, last = (drcv[1, corner, 0:1, :] for corner in along[side])
        tip = jnp.where(sub32 == 0, first, jnp.where(sub32 == 31, last, 0.0))
        outside[side] = outside[side] + w_out[side] * tip

    level = 4.0 * depth + up + down
    for k in range(ROWS // CHUNK):
        lo = k * CHUNK
        base_ref[lo : lo + CHUNK, :] = sweep(v0_ref, lo, CHUNK)
    for side in range(4):
        add_layer(base_ref, side, w_in[side] * outside[side])
    for k in range(ROWS // CHUNK):
        lo = k * CHUNK
        v1_ref[PAD + lo : PAD + lo + CHUNK, :] = 0.2 + r_ref[lo : lo + CHUNK, :] * level
    for k in range(ROWS // CHUNK):
        lo = k * CHUNK
        unit_ref[lo : lo + CHUNK, :] = sweep(v1_ref, lo, CHUNK, forced=False)
    w_next = [
        depth * r_ref[32:64, :],
        depth * r_ref[ROWS - 64 : ROWS - 32, :],
        depth * r_ref[pl.ds(1, 32, stride=32), :],
        depth * r_ref[pl.ds(30, 32, stride=32), :],
    ]

    gather_above()
    pl.semaphore_wait(ring.at[2], 2)
    gather_middle(0, ga1, ga2)
    gather_middle(1, gb1, gb2)
    gather_end(0, ga2)
    columns = coarse_factor(ga2, w0, n0)

    gather_end(1, gb2)
    total = jnp.zeros((8, 128), f32)
    for c in range(4):
        for p in range(2):
            total = total + columns[c, p] * gb2[pl.ds(8 * p + c, 8, stride=16), :]
    line = jnp.sum(total, axis=0, keepdims=True)
    line = jnp.where(iota((8, 128), 1) % 8 == iota((8, 128), 0), line, 0.0)
    near = jnp.sum(line, axis=1, keepdims=True) / ztotal
    near = jnp.broadcast_to(near, (8, 128))
    e = [near[k : k + 1, :] for k in range(8)]
    e0 = (own_res / ztotal + 32.0 * (e[0] + e[1] + e[2] + e[3])) / (128.0 + own_drag)
    edge, inner = [], []
    for side in range(4):
        first, last = (e[4 + corner] - e[side] for corner in along[side])
        jump = jnp.where(sub32 == 0, first, jnp.where(sub32 == 31, last, 0.0))
        beyond = (0.2 + r_out[side] * level) * e[side] + w_out[side] * ((e0 - e[side]) + jump)
        d = w_in[side] * (e[side] - e0)
        near = jnp.where(sub32 == 0, 0.0, pltpu.roll(d, 1, 0)) + jnp.where(sub32 == 31, 0.0, pltpu.roll(d, 31, 0))
        vert = up * pltpu.roll(d, 127, 1) + down * pltpu.roll(d, 1, 1)
        edge.append(0.2 * d + w_in[side] * (near + beyond) + layer(r_ref, side) * vert)
        inner.append(w_next[side] * d)
    for k in range(ROWS // CHUNK):
        lo = k * CHUNK
        out_ref[lo : lo + CHUNK, :] = base_ref[lo : lo + CHUNK, :] + e0 * unit_ref[lo : lo + CHUNK, :]
    out_ref[32:64, :] = out_ref[32:64, :] + inner[0]
    out_ref[ROWS - 64 : ROWS - 32, :] = out_ref[ROWS - 64 : ROWS - 32, :] + inner[1]
    for at, part in ((1, inner[2]), (30, inner[3])):
        out_ref[pl.ds(at, 32, stride=32), :] = out_ref[pl.ds(at, 32, stride=32), :] + part
    for side in range(4):
        add_layer(out_ref, side, edge[side])

    for there, copy, _ in sent_a + sent_b:
        pl.when(there)(copy.wait_send)
    gather_close(0, ga1, ga2)
    gather_close(1, gb1, gb2)


def local(forcing, classes, drag, depth):
    hbm = pl.BlockSpec(memory_space=pltpu.HBM)
    field = pltpu.VMEM((ROWS, 128), f32)
    padded = pltpu.VMEM((ROWS + 2 * PAD, 128), f32)
    args = (forcing.reshape(ROWS, 128), classes, drag, depth.reshape(1, 128))
    out = pl.pallas_call(
        kernel,
        out_shape=pltpu.VMEM((ROWS, 128), f32),
        in_specs=[hbm] * 4,
        out_specs=pl.BlockSpec(memory_space=pltpu.VMEM),
        scratch_shapes=[
            field, pltpu.VMEM((32, 32), jnp.int32), pltpu.SMEM((4,), f32), pltpu.VMEM((1, 128), f32),
            field, field, padded, padded, field, field,
            pltpu.VMEM((16, 128), f32),
            pltpu.VMEM((NN, 128), f32), pltpu.VMEM((8 * NW, 128), f32),
            pltpu.VMEM((NN, 128), f32), pltpu.VMEM((8 * NW, 128), f32),
            pltpu.VMEM((4, 72, 128), f32), pltpu.VMEM((4, 72, 128), f32),
            pltpu.VMEM((4, 64, 128), f32), pltpu.VMEM((4, 64, 128), f32),
            pltpu.VMEM((2, 4, 8, 128), f32), pltpu.VMEM((2, 4, 8, 128), f32),
            pltpu.SemaphoreType.DMA((4,)), pltpu.SemaphoreType.DMA((4,)), pltpu.SemaphoreType.DMA((4,)),
            pltpu.SemaphoreType.DMA((8,)), pltpu.SemaphoreType.DMA((8,)),
            pltpu.SemaphoreType.DMA((8,)), pltpu.SemaphoreType.DMA((8,)), pltpu.SemaphoreType.REGULAR,
            pltpu.SemaphoreType.REGULAR((3,)),
        ],
        compiler_params=pltpu.CompilerParams(
            collective_id=0, has_side_effects=True, vmem_limit_bytes=40 * 1024 * 1024
        ),
        name="vcycle",
    )(*(pltpu.with_memory_space_constraint(a, pltpu.HBM) for a in args))
    return out.reshape(forcing.shape)


def solution(mesh):
    in_specs = (P("wide", "narrow", None), P("wide", "narrow"), P(), P())
    out_specs = P("wide", "narrow", None)
    return jax.shard_map(local, mesh=mesh, in_specs=in_specs, out_specs=out_specs, check_vma=False)
```

```python
import math
import functools
import jax
import jax.numpy as jnp
from jax import lax
from jax.experimental import pallas as pl
from jax.experimental.pallas import tpu as pltpu
from jax.sharding import PartitionSpec as P

f32 = jnp.float32
MESH = pl.DeviceIdType.MESH
ROWS = 1024
PAD = 32
CHUNK = 256
NW, NN = 16, 64

RHO = 32.0 * (2.0 * math.cos(math.pi / 17) + 2.0 * math.cos(math.pi / 65)) / 128.0199
HALF = 1.0 - RHO * RHO / 2.0
RHO2 = RHO * RHO / 2.0 / HALF
ROOT = math.sqrt(1.0 - RHO2 * RHO2)
SIG = (1.0 - ROOT) / RHO2
SCALE = 2.0 / (HALF * ROOT)
TRIPS = 16


def iota(shape, dim):
    return lax.broadcasted_iota(jnp.int32, shape, dim)


def layer(ref, side, base=0):
    if side == 0:
        return ref[pl.ds(base, 32), :]
    if side == 1:
        return ref[pl.ds(base + ROWS - 32, 32), :]
    return ref[pl.ds(base + (0 if side == 2 else 31), 32, stride=32), :]


def add_layer(ref, side, value, base=0):
    if side == 0:
        ref[pl.ds(base, 32), :] = ref[pl.ds(base, 32), :] + value
    elif side == 1:
        at = base + ROWS - 32
        ref[pl.ds(at, 32), :] = ref[pl.ds(at, 32), :] + value
    else:
        at = base + (0 if side == 2 else 31)
        ref[pl.ds(at, 32, stride=32), :] = ref[pl.ds(at, 32, stride=32), :] + value


CORNERS = ((0, 2), (0, 3), (1, 2), (1, 3))
CORNER_ROW = (0, 31, ROWS - 32, ROWS - 1)


def coarse_factor(d_ref, w0, n0):
    lane, sub = iota((8, 128), 1), iota((8, 128), 0)
    z, r = lane // 8, lane % 8
    q = {}
    for c in range(4):
        for p in range(2):
            q[c, p] = 32.0 / (128.0 + d_ref[pl.ds(8 * p + c, 8, stride=16), :])

    def shifted(v, cols):
        if cols == 0:
            return v
        rolled = pltpu.roll(v, (-8 * cols) % 128, 1)
        inside = (z + cols >= 0) & (z + cols < 16)
        return jnp.where(inside, rolled, 0.0)

    for c in list(range(-8, 0)) + list(range(4, 12)):
        for p in range(2):
            q[c, p] = shifted(q[c % 4, p], c // 4)

    def gather(x, c, p):
        other = x[c, 1 - p]
        if p == 0:
            near = jnp.where(sub == 0, 0.0, pltpu.roll(other, 1, 0))
        else:
            near = jnp.where(sub == 7, 0.0, pltpu.roll(other, 7, 0))
        return (x[c - 1, p] + x[c + 1, p]) + (other + near)

    dw = jnp.where(r == 0, -1, jnp.where(r == 1, 1, jnp.where(r < 4, 0, jnp.where(r < 6, -1, 1))))
    dn = jnp.where(r < 2, 0, jnp.where(r == 2, -1, jnp.where(r == 3, 1, jnp.where(r % 2 == 0, -1, 1))))
    want_w, want_n = w0 + dw, n0 + dn - 4 * z

    def unit(c, p):
        hit = (2 * sub + p == want_w) & (want_n == c)
        return jnp.where(hit, q[c, p] * (1.0 / 32.0), 0.0)

    def color(c, which):
        return (c + which) % 2

    b = {}
    for c in range(-1, 5):
        b[c, color(c, 1)] = unit(c, color(c, 1))
    g = {}
    for c in range(4):
        p = color(c, 0)
        g[c] = unit(c, p) + q[c, p] * gather(b, c, p)

    c_two, c_cur, c_old = 4.0 * SIG / (RHO * RHO), 2.0 * SIG, SIG * SIG

    def trip(it, carry):
        acc, cur, old = carry
        x, o = {}, {}
        for c in range(-8, 12):
            x[c, color(c, 0)] = shifted(cur[c % 4], c // 4)
            if -6 <= c < 10:
                o[c] = shifted(old[c % 4], c // 4)
        acc = list(acc)
        first = jnp.where(it == 0, 0.5, 1.0).astype(f32)
        for app in range(4):
            lo, hi = -8 + 2 * app, 12 - 2 * app
            y = {}
            for c in range(lo + 1, hi - 1):
                p = color(c, 1)
                y[c, p] = q[c, p] * gather(x, c, p)
            new = {}
            for c in range(lo + 2, hi - 2):
                p = color(c, 0)
                t = (c_two * q[c, p]) * gather(y, c, p) - c_cur * x[c, p]
                if app == 0:
                    t = first * t
                new[c, p] = t - c_old * o[c]
            o = {c: x[c, color(c, 0)] for c in range(lo + 2, hi - 2)}
            x = new
            for c in range(4):
                acc[c] = acc[c] + x[c, color(c, 0)]
        return tuple(acc), tuple(x[c, color(c, 0)] for c in range(4)), tuple(o[c] for c in range(4))

    g = tuple(g[c] for c in range(4))
    zero = jnp.zeros((8, 128), f32)
    acc, _, _ = lax.fori_loop(0, TRIPS, trip, (tuple(0.5 * v for v in g), g, (zero,) * 4))
    x = {(c, color(c, 0)): SCALE * acc[c] for c in range(4)}
    x[-1, color(-1, 0)] = shifted(x[3, color(3, 0)], -1)
    x[4, color(4, 0)] = shifted(x[0, color(0, 0)], 1)
    out = {}
    for c in range(4):
        out[c, color(c, 0)] = x[c, color(c, 0)]
        p = color(c, 1)
        out[c, p] = b[c, p] + q[c, p] * gather(x, c, p)

    parts = {}
    for c in range(4):
        for p in range(2):
            flip = out[c, 1 - p]
            low = jnp.where(sub == 0, 0.0, pltpu.roll(flip, 1, 0)) if p == 0 else flip
            high = flip if p == 0 else jnp.where(sub == 7, 0.0, pltpu.roll(flip, 7, 0))
            left = out[c - 1, p] if c > 0 else shifted(out[3, p], -1)
            right = out[c + 1, p] if c < 3 else shifted(out[0, p], 1)
            parts[c, p] = [out[c, p]] + [beyond - out[c, p] for beyond in (low, high, left, right)]
    return parts


def kernel(
    f_hbm, cls_hbm, drag_hbm, depth_hbm, out_ref,
    f_ref, cls_ref, drag_ref, depth_ref,
    r_ref, s_ref, v0_ref, v1_ref, base_ref, unit_ref, pick_ref,
    row, ga1, ga2, gb1, gb2, snd_a, rcv_a, snd_b, rcv_b, dsnd, drcv,
    load, gs, gr, hs, hr, ds, dr, credit, ring,
):
    w0, n0 = lax.axis_index("wide"), lax.axis_index("narrow")
    z0, x0 = n0 // 4, n0 % 4

    loads = [
        pltpu.make_async_copy(src, dst, load.at[k])
        for k, (src, dst) in enumerate(
            ((cls_hbm, cls_ref), (drag_hbm, drag_ref), (depth_hbm, depth_ref), (f_hbm, f_ref))
        )
    ]
    for c in loads:
        c.start()

    bar = pltpu.get_barrier_semaphore()

    def greet(w, n):
        pl.semaphore_signal(bar, inc=1, device_id=(w, n), device_id_type=MESH)

    def beside_x(p):
        return z0 * 4 + (x0 + p) % 4

    sides = ((w0 - 1, n0), (w0 + 1, n0), (w0, n0 - 1), (w0, n0 + 1))
    exist = (w0 > 0, w0 < NW - 1, n0 > 0, n0 < NN - 1)
    diags = tuple((sides[a][0], sides[b][1]) for a, b in CORNERS)
    dexist = tuple(exist[a] & exist[b] for a, b in CORNERS)

    y0, c0 = w0 // 2, w0 % 2
    ring_next = (((y0 + 1) % 8) * 2 + c0, ((y0 + 7) % 8) * 2 + c0)

    def relay(k):
        for w in ring_next:
            pl.semaphore_signal(ring.at[k], inc=1, device_id=(w, n0), device_id_type=MESH)

    def greet_above(n, _):
        greet(w0, n)
        return 0

    for p in range(1, 4):
        greet(w0, beside_x(p))
    pl.when((x0 == 0) & (z0 > 0))(functools.partial(greet, w0, n0 - 1))
    greet(y0 * 2 + (1 - c0), n0)
    for dy in (1, 7):
        for c in (0, 1):
            greet(((y0 + dy) % 8) * 2 + c, n0)
    lax.fori_loop(4 * z0 + 4, NN, greet_above, 0)

    for side in range(4):

        @pl.when(jnp.logical_not(exist[side]))
        def _(side=side):
            rcv_a[side] = jnp.zeros((32, 128), f32)
            rcv_b[side] = jnp.zeros((96, 128), f32)

    for corner in range(4):

        @pl.when(jnp.logical_not(dexist[corner]))
        def _(corner=corner):
            drcv[corner] = jnp.zeros((8, 128), f32)

    zpad = jnp.zeros((PAD, 128), f32)
    for ref in (v0_ref, v1_ref):
        ref[0:PAD, :] = zpad
        ref[PAD + ROWS : PAD + ROWS + PAD, :] = zpad

    for c in loads[:3]:
        c.wait()
    lane = iota((1, 128), 1)
    depth = depth_ref[...]
    link = jnp.where(lane == 127, 0.0, 2.0 / (depth + pltpu.roll(depth, 127, 1)))
    up, down = link, pltpu.roll(link, 1, 1)
    ztotal = jnp.sum(depth, axis=1, keepdims=True)
    drags = [drag_ref[c] for c in range(4)]
    tables = [0.8 / (depth * (4.0 + d) + up + down) for d in drags]

    kinds = cls_ref[...]

    def sweep(src, lo, n, forced=True):
        jpos = iota((n, 128), 0) % 32
        c = src[PAD + lo : PAD + lo + n, :]
        near = src[lo : lo + n, :] + src[2 * PAD + lo : 2 * PAD + lo + n, :]
        near = near + jnp.where(jpos == 0, 0.0, src[PAD + lo - 1 : PAD + lo - 1 + n, :])
        near = near + jnp.where(jpos == 31, 0.0, src[PAD + lo + 1 : PAD + lo + 1 + n, :])
        force = depth * near + (up * pltpu.roll(c, 127, 1) + down * pltpu.roll(c, 1, 1))
        if forced:
            force = f_ref[lo : lo + n, :] + force
        return 0.2 * c + r_ref[lo : lo + n, :] * force

    def exchange(snd, rcv, base, corners):
        copies = []
        for side, t in enumerate(sides):
            copy = pltpu.make_async_remote_copy(
                src_ref=snd.at[side], dst_ref=rcv.at[side ^ 1], send_sem=hs.at[base + side],
                recv_sem=hr.at[base + (side ^ 1)], device_id=t, device_id_type=MESH,
            )
            mirror = pltpu.make_async_remote_copy(
                src_ref=snd.at[side], dst_ref=rcv.at[side], send_sem=hs.at[base + side],
                recv_sem=hr.at[base + side], device_id=t, device_id_type=MESH,
            )
            copies.append((exist[side], copy, mirror))
        for corner, t in enumerate(diags if corners else ()):
            copy = pltpu.make_async_remote_copy(
                src_ref=dsnd.at[corner, pl.ds(0, 1)], dst_ref=drcv.at[3 - corner, pl.ds(0, 1)],
                send_sem=ds.at[corner], recv_sem=dr.at[3 - corner], device_id=t, device_id_type=MESH,
            )
            mirror = pltpu.make_async_remote_copy(
                src_ref=dsnd.at[corner, pl.ds(0, 1)], dst_ref=drcv.at[corner, pl.ds(0, 1)],
                send_sem=ds.at[corner], recv_sem=dr.at[corner], device_id=t, device_id_type=MESH,
            )
            copies.append((dexist[corner], copy, mirror))
        for there, copy, _ in copies:
            pl.when(there)(copy.start)
        return copies

    def arrive(copies):
        for there, _, mirror in copies:
            pl.when(there)(mirror.wait_recv)

    s2d = jnp.where(kinds == 0, drags[0], jnp.where(kinds == 1, drags[1], jnp.where(kinds == 2, drags[2], drags[3])))
    own_drag = jnp.sum(jnp.sum(s2d, axis=0, keepdims=True), axis=1, keepdims=True) * (1.0 / ROWS)
    row[0:1, :] = jnp.broadcast_to(own_drag, (1, 128))
    hello = 4 * z0 + 3 + 5 + jnp.where((x0 == 3) & (z0 < 15), 1, 0)
    pl.semaphore_wait(bar, hello)
    relay(0)

    sub16, lane16 = iota((16, 128), 0), iota((16, 128), 1)
    mine = x0 * 16 + z0

    def drain(buf, rows, sem):
        pltpu.make_async_copy(buf.at[pl.ds(0, rows)], buf.at[pl.ds(0, rows)], sem).wait()

    def narrow_send(k, buf, n):
        pltpu.make_async_remote_copy(
            src_ref=row.at[pl.ds(8 * k, 1)], dst_ref=buf.at[pl.ds(mine, 1)], send_sem=gs.at[2 * k],
            recv_sem=gr.at[2 * k], device_id=(w0, n), device_id_type=MESH,
        ).start()

    def gather_start(k, buf, lo, hi, last=True):
        def send(n, _):
            narrow_send(k, buf, n)
            return 0

        lax.fori_loop(lo, hi, send, 0)
        if last:
            buf[pl.ds(mine, 1), :] = row[8 * k : 8 * k + 1, :]
            for p in range(1, 4):
                narrow_send(k, buf, beside_x(p))

    def gather_above():
        @pl.when(z0 < 15)
        def _():
            pl.semaphore_wait(credit, 4 * (15 - z0))


        def send(n, _):
            narrow_send(0, ga1, n)
            narrow_send(1, gb1, n)
            return 0

        lax.fori_loop(4 * z0 + 4, NN, send, 0)

    def gather_middle(k, buf, buf2):
        drain(buf, NN - 1, gr.at[2 * k])
        at = pl.multiple_of(w0 * 8, 8)
        rows = [
            jnp.sum(jnp.where(lane16 // 8 == sub16, buf[16 * x : 16 * x + 16, :], 0.0), axis=0, keepdims=True)
            for x in range(4)
        ]
        buf2[pl.ds(at, 4), :] = jnp.concatenate(rows, axis=0)

        def send(p, _):
            pltpu.make_async_remote_copy(
                src_ref=buf2.at[pl.ds(at, 4)], dst_ref=buf2.at[pl.ds(at, 4)], send_sem=gs.at[2 * k + 1],
                recv_sem=gr.at[2 * k + 1], device_id=((w0 + p) % NW, n0), device_id_type=MESH,
            ).start()
            return 0

        lax.fori_loop(1, NW, send, 0)

    def gather_end(k, buf2):
        drain(buf2, 4 * (NW - 1), gr.at[2 * k + 1])

    def gather_close(k, buf, buf2):
        drain(buf, NN - 1, gs.at[2 * k])
        drain(buf2, 4 * (NW - 1), gs.at[2 * k + 1])

    urgent = jnp.minimum(4 * z0, 16)
    gather_start(0, ga1, 0, urgent, last=False)
    cf = kinds.astype(f32)
    eye = jnp.where(iota((32, 32), 0) == iota((32, 32), 1), 1.0, 0.0).astype(f32)
    ones = jnp.ones((32, 128), f32)
    loads[3].wait()
    sum_f = jnp.zeros((8, 128), f32)
    for k in range(ROWS // CHUNK):
        ni = CHUNK // 32
        spread = (cf[k * ni : (k + 1) * ni][:, None, :] * eye[None]).reshape(CHUNK, 32)
        kind = jnp.dot(spread, ones, preferred_element_type=f32)
        is0, is1, is2 = kind < 0.5, kind < 1.5, kind < 2.5
        rr = jnp.where(is0, tables[0], jnp.where(is1, tables[1], jnp.where(is2, tables[2], tables[3])))
        ss = jnp.where(is0, drags[0], jnp.where(is1, drags[1], jnp.where(is2, drags[2], drags[3])))
        f = f_ref[k * CHUNK : (k + 1) * CHUNK, :]
        r_ref[k * CHUNK : (k + 1) * CHUNK, :] = rr
        s_ref[k * CHUNK : (k + 1) * CHUNK, :] = ss
        v0_ref[PAD + k * CHUNK : PAD + (k + 1) * CHUNK, :] = rr * f
        sum_f = sum_f + jnp.sum(f.reshape(CHUNK // 8, 8, 128), axis=0)

    for side in range(4):
        snd_a[side] = layer(v0_ref, side, PAD)
    sent_a = exchange(snd_a, rcv_a, 0, False)
    gather_start(0, ga1, urgent, 4 * z0)

    def give_credit(n, _):
        pl.semaphore_signal(credit, inc=1, device_id=(w0, n), device_id_type=MESH)
        return 0

    lax.fori_loop(0, 4 * z0, give_credit, 0)

    sum_s = jnp.zeros((8, 128), f32)
    for k in range(ROWS // CHUNK):
        lo = k * CHUNK
        v = sweep(v0_ref, lo, CHUNK)
        v1_ref[PAD + lo : PAD + lo + CHUNK, :] = v
        sum_s = sum_s + jnp.sum((s_ref[lo : lo + CHUNK, :] * v).reshape(CHUNK // 8, 8, 128), axis=0)

    pl.semaphore_wait(ring.at[0], 2)
    relay(1)
    arrive(sent_a)
    pl.semaphore_wait(ring.at[1], 2)
    relay(2)
    w_in = [depth * layer(r_ref, side) for side in range(4)]
    sub32 = iota((32, 128), 0)
    drained = jnp.sum(sum_s, axis=0, keepdims=True)
    for side in range(4):
        delta = w_in[side] * rcv_a[side]
        drained = drained + jnp.sum(layer(s_ref, side) * delta, axis=0, keepdims=True)
        add_layer(v1_ref, side, delta, PAD)
    own_part = jnp.sum(sum_f, axis=0, keepdims=True) - depth * drained
    leaves = [depth * jnp.sum(layer(v1_ref, side, PAD), axis=0, keepdims=True) for side in range(4)]
    sub8, lane8 = iota((8, 128), 0), iota((8, 128), 1)
    stack = jnp.where(sub8 == 0, own_part, 0.0)
    for side in range(4):
        stack = jnp.where(sub8 == side + 1, leaves[side], stack)
    five = jnp.broadcast_to(jnp.sum(stack, axis=1, keepdims=True), (8, 128))
    row[8:9, :] = jnp.sum(jnp.where(lane8 % 8 == sub8, five, 0.0), axis=0, keepdims=True)
    gather_start(1, gb1, 0, 4 * z0)

    for k in range(ROWS // CHUNK):
        v0_ref[PAD + k * CHUNK : PAD + (k + 1) * CHUNK, :] = sweep(v1_ref, k * CHUNK, CHUNK)
    for side in range(4):
        snd_b[side, 0:32, :] = layer(v1_ref, side, PAD)
        snd_b[side, 32:64, :] = layer(v0_ref, side, PAD)
        snd_b[side, 64:96, :] = layer(r_ref, side)
    for corner, at in enumerate(CORNER_ROW):
        dsnd[corner, 0:1, :] = v1_ref[PAD + at : PAD + at + 1, :]
    sent_b = exchange(snd_b, rcv_b, 4, True)

    arrive(sent_b)
    r_out = [rcv_b[side, 64:96, :] for side in range(4)]
    w_out = [depth * r_out[side] for side in range(4)]
    res = own_part
    for side in range(4):
        res = res - leaves[side] + depth * jnp.sum(rcv_b[side, 0:32, :], axis=0, keepdims=True)
    own_res = jnp.sum(res, axis=1, keepdims=True)
    outside = []
    for side in range(4):
        add_layer(v0_ref, side, w_in[side] * rcv_b[side, 0:32, :], PAD)
        outside.append(rcv_b[side, 32:64, :] + w_out[side] * layer(v1_ref, side, PAD))
    along = ((0, 1), (2, 3), (0, 2), (1, 3))
    for side in range(4):
        first, last = (drcv[corner, 0:1, :] for corner in along[side])
        tip = jnp.where(sub32 == 0, first, jnp.where(sub32 == 31, last, 0.0))
        outside[side] = outside[side] + w_out[side] * tip

    level = 4.0 * depth + up + down
    for k in range(ROWS // CHUNK):
        lo = k * CHUNK
        base_ref[lo : lo + CHUNK, :] = sweep(v0_ref, lo, CHUNK)
    for side in range(4):
        add_layer(base_ref, side, w_in[side] * outside[side])
    for k in range(ROWS // CHUNK):
        lo = k * CHUNK
        v1_ref[PAD + lo : PAD + lo + CHUNK, :] = 0.2 + r_ref[lo : lo + CHUNK, :] * level
    for k in range(ROWS // CHUNK):
        lo = k * CHUNK
        unit_ref[lo : lo + CHUNK, :] = sweep(v1_ref, lo, CHUNK, forced=False)
    w_next = [
        depth * r_ref[32:64, :],
        depth * r_ref[ROWS - 64 : ROWS - 32, :],
        depth * r_ref[pl.ds(1, 32, stride=32), :],
        depth * r_ref[pl.ds(30, 32, stride=32), :],
    ]

    for k in range(5):
        source, target = iota((128, 128), 0), iota((128, 128), 1)
        pick_ref[:, 128 * k : 128 * k + 128] = jnp.where(source == target // 8 * 8 + k, 1.0, 0.0).astype(f32)

    gather_above()
    pl.semaphore_wait(ring.at[2], 2)
    gather_middle(0, ga1, ga2)
    gather_middle(1, gb1, gb2)
    gather_end(0, ga2)
    parts = coarse_factor(ga2, w0, n0)

    gather_end(1, gb2)
    gathered = jnp.concatenate([gb2[pl.ds(8 * p + c, 8, stride=16), :] for c in range(4) for p in range(2)], axis=0)
    wide = jnp.dot(gathered, pick_ref[...], precision=lax.Precision.HIGHEST, preferred_element_type=f32)
    total = jnp.zeros((8, 128), f32)
    for c in range(4):
        for p in range(2):
            at = 8 * (2 * c + p)
            for k in range(5):
                total = total + parts[c, p][k] * wide[at : at + 8, 128 * k : 128 * k + 128]
    line = jnp.sum(total, axis=0, keepdims=True)
    line = jnp.where(iota((8, 128), 1) % 8 == iota((8, 128), 0), line, 0.0)
    near = jnp.sum(line, axis=1, keepdims=True) / ztotal
    near = jnp.broadcast_to(near, (8, 128))
    e = [near[k : k + 1, :] for k in range(8)]
    e0 = (own_res / ztotal + 32.0 * (e[0] + e[1] + e[2] + e[3])) / (128.0 + own_drag)
    edge, inner = [], []
    for side in range(4):
        first, last = (e[4 + corner] - e[side] for corner in along[side])
        jump = jnp.where(sub32 == 0, first, jnp.where(sub32 == 31, last, 0.0))
        beyond = (0.2 + r_out[side] * level) * e[side] + w_out[side] * ((e0 - e[side]) + jump)
        d = w_in[side] * (e[side] - e0)
        near = jnp.where(sub32 == 0, 0.0, pltpu.roll(d, 1, 0)) + jnp.where(sub32 == 31, 0.0, pltpu.roll(d, 31, 0))
        vert = up * pltpu.roll(d, 127, 1) + down * pltpu.roll(d, 1, 1)
        edge.append(0.2 * d + w_in[side] * (near + beyond) + layer(r_ref, side) * vert)
        inner.append(w_next[side] * d)
    for k in range(ROWS // CHUNK):
        lo = k * CHUNK
        out_ref[lo : lo + CHUNK, :] = base_ref[lo : lo + CHUNK, :] + e0 * unit_ref[lo : lo + CHUNK, :]
    out_ref[32:64, :] = out_ref[32:64, :] + inner[0]
    out_ref[ROWS - 64 : ROWS - 32, :] = out_ref[ROWS - 64 : ROWS - 32, :] + inner[1]
    for at, part in ((1, inner[2]), (30, inner[3])):
        out_ref[pl.ds(at, 32, stride=32), :] = out_ref[pl.ds(at, 32, stride=32), :] + part
    for side in range(4):
        add_layer(out_ref, side, edge[side])

    for there, copy, _ in sent_a + sent_b:
        pl.when(there)(copy.wait_send)
    gather_close(0, ga1, ga2)
    gather_close(1, gb1, gb2)


def local(forcing, classes, drag, depth):
    hbm = pl.BlockSpec(memory_space=pltpu.HBM)
    field = pltpu.VMEM((ROWS, 128), f32)
    padded = pltpu.VMEM((ROWS + 2 * PAD, 128), f32)
    args = (forcing.reshape(ROWS, 128), classes, drag, depth.reshape(1, 128))
    out = pl.pallas_call(
        kernel,
        out_shape=pltpu.VMEM((ROWS, 128), f32),
        in_specs=[hbm] * 4,
        out_specs=pl.BlockSpec(memory_space=pltpu.VMEM),
        scratch_shapes=[
            field, pltpu.VMEM((32, 32), jnp.int32), pltpu.SMEM((4,), f32), pltpu.VMEM((1, 128), f32),
            field, field, padded, padded, field, field, pltpu.VMEM((128, 640), f32),
            pltpu.VMEM((16, 128), f32),
            pltpu.VMEM((NN, 128), f32), pltpu.VMEM((8 * NW, 128), f32),
            pltpu.VMEM((NN, 128), f32), pltpu.VMEM((8 * NW, 128), f32),
            pltpu.VMEM((4, 32, 128), f32), pltpu.VMEM((4, 32, 128), f32),
            pltpu.VMEM((4, 96, 128), f32), pltpu.VMEM((4, 96, 128), f32),
            pltpu.VMEM((4, 8, 128), f32), pltpu.VMEM((4, 8, 128), f32),
            pltpu.SemaphoreType.DMA((4,)), pltpu.SemaphoreType.DMA((4,)), pltpu.SemaphoreType.DMA((4,)),
            pltpu.SemaphoreType.DMA((8,)), pltpu.SemaphoreType.DMA((8,)),
            pltpu.SemaphoreType.DMA((4,)), pltpu.SemaphoreType.DMA((4,)), pltpu.SemaphoreType.REGULAR,
            pltpu.SemaphoreType.REGULAR((3,)),
        ],
        compiler_params=pltpu.CompilerParams(
            collective_id=0, has_side_effects=True, vmem_limit_bytes=40 * 1024 * 1024
        ),
        name="vcycle",
    )(*(pltpu.with_memory_space_constraint(a, pltpu.HBM) for a in args))
    return out.reshape(forcing.shape)


def solution(mesh):
    in_specs = (P("wide", "narrow", None), P("wide", "narrow"), P(), P())
    out_specs = P("wide", "narrow", None)
    return jax.shard_map(local, mesh=mesh, in_specs=in_specs, out_specs=out_specs, check_vma=False)
```
